32 devices in a mesh: wide: 8 (over y, x, core), narrow: 4 (over z).
Axes of the slice: x: 2, y: 2, z: 4, core: 2. Of those that a mesh axis runs over, the one named last changes fastest.
Arguments:
- amplitude: float32 [2048, 256], P(('wide', 'narrow')), may hold values from -6 to 6
- tilt: float32 [3, 2048], P(None, ('wide', 'narrow')), may hold values from -3.140625 to 3.140625
- owner: int32 [2048, 1], P(('wide', 'narrow')), may hold values from 0 to 7; in each aligned block of 64 rows (0 to 63, 64 to 127, ...) at most 24 rows name the same one
- row_offset: int32 [2048], P(('wide', 'narrow')), may hold values from 0 to 496
- col_offset: int32 [2048], P(('wide', 'narrow')), may hold values from 0 to 240
Outputs:
- hologram: float32 [2, 2048, 2048], P(None, 'narrow', 'wide')
The draws below stay inside these ranges and needn't reach their ends.
Inputs may be any that keep to these rules, and one draw needn't show every extreme that they name: `owner`: among the 64 facets of one device no tile column is named more than 24 times, and on some device one column is named exactly 24 times.
All inputs are finite; a program needn't handle non-finite values.
Results may differ from the reference program's by a relative error of at most 0.0085.
Values may be sent and summed in bfloat16 or wider, within the bound.
A program may use at most 64 MiB of HBM per device.

```python
import math
import jax
import jax.numpy as jnp
import numpy as np
from jax import lax

TH = 512
TW = 256
FACET = 16
FAC_DEV = 64
CAP = 24
DEPTH = 1280
FACETS = 2048
NY = 2048
NX = 2048
N_WIDE = 8
N_NARROW = 4


def with_ends(array, stream_key, low, top_value):
    longest = array.shape.index(max(array.shape))
    spots = []
    for shift in (0, 1):
        where = [jax.random.randint(jax.random.fold_in(stream_key, axis), (), 0, length) for axis, length in enumerate(array.shape)]
        where[longest] = (where[longest] + shift) % array.shape[longest]
        spots.append(tuple(where))
    return array.at[spots[0]].set(low).at[spots[1]].set(top_value)


def block_levels(key, extent, split, low, top_value):
    factor_of = 1.0
    for axis_at, blocks in split:
        steps = jax.random.uniform(jax.random.fold_in(jax.random.fold_in(key, 6), axis_at), (blocks,), jnp.float32, low / len(split), top_value / len(split))
        factor_of = factor_of * jnp.repeat(jnp.exp(steps), extent[axis_at] // blocks).reshape((-1,) + (1,) * (len(extent) - 1 - axis_at))
    return factor_of


def deal_out(key, own, number, rows, count, top, bound, slope):
    sequence = jax.random.permutation(key, count)
    packed, ordinary = portions_of(count, rows * top, bound, slope, True), portions_of(count, rows * top, bound, slope, False)
    places = jnp.arange(count)

    def named(lengths, turn):
        used = int((lengths > 0).sum())
        fixed = max(1, used // 4)
        moved = fixed + (places - fixed + turn * (used - fixed)) % max(1, count - fixed)
        return jnp.zeros((count,), jnp.int32).at[sequence[jnp.where(places < fixed, places, moved)]].set(jnp.asarray(lengths, jnp.int32))

    lengths = jnp.where(number % 4 == 0, named(packed, number // 4), named(ordinary, number - number // 4 - 1))
    mixed = jax.random.permutation(jax.random.fold_in(own, 3), count)
    source_of, receiver = mixed[0:count // 2 * 2:2], mixed[1:count // 2 * 2:2]
    margin = jnp.minimum(lengths[source_of] - 1, bound - lengths[receiver]) // 2
    margin = jnp.where((source_of == sequence[0]) | (receiver == sequence[0]) | (lengths[receiver] == 0), 0, jnp.maximum(margin, 0))
    moved = jax.random.randint(jax.random.fold_in(own, 4), (count // 2,), 0, 1 << 20) % (margin + 1)
    lengths = lengths.at[source_of].add(-moved).at[receiver].add(moved)
    labels = jnp.searchsorted(jnp.cumsum(lengths), jnp.arange(rows * top), side="right").astype(jnp.int32)
    table = labels.reshape(top, rows).T
    table = table[jax.random.permutation(jax.random.fold_in(own, 1), rows)]
    turn = jax.random.randint(jax.random.fold_in(own, 2), (rows, 1), 0, top)
    return jnp.take_along_axis(table, (jnp.arange(top)[None, :] + turn) % top, axis=1)


def portions_of(count, total, limit, slope, full):
    weights = [(1 << 20) // math.isqrt(standing ** slope) + 1 for standing in range(1, count + 1)]
    largest = limit if full else min(limit, max(-(-total // count), total * weights[0] // sum(weights)))
    least = 1 if total - largest >= count - 1 else 0
    given, rest = [largest] + [least] * (count - 1), total - largest - least * (count - 1)
    while rest > 0:
        candidates = [i for i in range(1, count) if given[i] < largest] or [i for i in range(1, count) if given[i] < limit]
        whole, left = sum([weights[i] for i in candidates]), rest
        for i in candidates:
            more = min(limit - given[i], max(1, left * weights[i] // whole), rest)
            given[i] = given[i] + more
            rest = rest - more
    return np.array(given)


def bell_draw(stream_key, shape, width, limit, cuts=(), held_as=jnp.bfloat16):
    entries = width * jax.random.normal(stream_key, shape, jnp.float32)
    if cuts:
        entries = entries * block_levels(stream_key, shape, cuts, -0.22, 0.18)
    return jnp.clip(entries, -limit, limit).astype(held_as)


def setup_inputs(seed: int = 0) -> dict:
    keys = jax.random.split(jax.random.key(seed), 6)
    amplitude = bell_draw(keys[0], (FACETS, FACET * FACET), 1.0, 6.0, ((0, 32),), jnp.float32)
    tilt = jnp.clip(jax.random.uniform(keys[1], (3, FACETS), jnp.float32, -3.140625, 3.140625), -3.140625, 3.140625)
    owner_keys = jax.random.split(jax.random.fold_in(keys[2], 1), FACETS // FAC_DEV)
    owner_turns = jax.random.permutation(jax.random.fold_in(keys[2], 3), FACETS // FAC_DEV)
    owner = jax.vmap(lambda own, number: deal_out(jax.random.fold_in(keys[2], 2), own, number, FAC_DEV, N_WIDE, 1, CAP, 2))(owner_keys, owner_turns).reshape((FACETS, 1))
    row_offset = with_ends(jax.random.randint(keys[3], (FACETS,), 0, TH - FACET + 1), jax.random.fold_in(keys[3], 1), 0, TH - FACET).astype(jnp.int32)
    col_offset = with_ends(jax.random.randint(keys[4], (FACETS,), 0, TW - FACET + 1), jax.random.fold_in(keys[4], 1), 0, TW - FACET).astype(jnp.int32)
    return dict(amplitude=amplitude, tilt=tilt, owner=owner, row_offset=row_offset, col_offset=col_offset)


reach_spread = 16.0

def dft_tables(length, spin_sign):
    position = jnp.arange(length, dtype=jnp.int32)
    product = position[:, None] * position[None, :] % length
    angles = product.astype(jnp.float32) * (2.0 * math.pi / length)
    return (jnp.cos(angles).astype(jnp.bfloat16), (spin_sign * jnp.sin(angles)).astype(jnp.bfloat16))

def signed_frequency(length):
    position = jnp.arange(length, dtype=jnp.int32)
    return (position + length // 2) % length - length // 2

def reach_weight(length, depth_cells, offset):
    travel = signed_frequency(length).astype(jnp.float32) * (depth_cells / (length * length))
    return jnp.exp(-(travel - offset) ** 2 / reach_spread)

def depth_phase(length, depth_cells):
    frequency = signed_frequency(length)
    turn_count = depth_cells * frequency * frequency % (2 * length * length)
    return turn_count.astype(jnp.float32) * (-math.pi / (length * length))

def render(amplitude, tilt, patch):
    position = jnp.arange(patch * patch, dtype=jnp.int32)
    row_pos = (position // patch).astype(jnp.float32)
    col_pos = (position % patch).astype(jnp.float32)
    phase = tilt[0][:, None] * row_pos[None, :] + tilt[1][:, None] * col_pos[None, :] + tilt[2][:, None]
    return ((amplitude * jnp.cos(phase)).astype(jnp.bfloat16), (amplitude * jnp.sin(phase)).astype(jnp.bfloat16))

def left_apply(table_r, table_i, real_part, imag_part):
    real_real = jnp.dot(table_r, real_part, preferred_element_type=jnp.float32)
    imag_imag = jnp.dot(table_i, imag_part, preferred_element_type=jnp.float32)
    real_imag = jnp.dot(table_r, imag_part, preferred_element_type=jnp.float32)
    imag_real = jnp.dot(table_i, real_part, preferred_element_type=jnp.float32)
    return (real_real - imag_imag, real_imag + imag_real)

def tile_right(real_part, imag_part, table_r, table_i):
    real_wide = real_part.astype(jnp.float32)
    imag_wide = imag_part.astype(jnp.float32)
    tab_r = table_r.astype(jnp.float32)
    tab_i = table_i.astype(jnp.float32)
    high = lax.Precision.HIGHEST
    real_real = jnp.einsum('ywk,kx->ywx', real_wide, tab_r, precision=high)
    imag_imag = jnp.einsum('ywk,kx->ywx', imag_wide, tab_i, precision=high)
    real_imag = jnp.einsum('ywk,kx->ywx', real_wide, tab_i, precision=high)
    imag_real = jnp.einsum('ywk,kx->ywx', imag_wide, tab_r, precision=high)
    return (real_real - imag_imag, real_imag + imag_real)

def reference(amplitude, tilt, owner, row_offset, col_offset):
    field_r, field_i = render(amplitude, tilt, FACET)
    position = jnp.arange(FACET * FACET, dtype=jnp.int32)
    band = jnp.arange(FACETS, dtype=jnp.int32) // FAC_DEV % N_NARROW
    rows_at = (band * TH + row_offset)[:, None] + (position // FACET)[None, :]
    cols_at = (owner[:, 0] * TW + col_offset)[:, None] + (position % FACET)[None, :]
    plane_r = jnp.zeros((NY, NX), jnp.float32).at[rows_at, cols_at].add(field_r.astype(jnp.float32)).astype(jnp.bfloat16)
    plane_i = jnp.zeros((NY, NX), jnp.float32).at[rows_at, cols_at].add(field_i.astype(jnp.float32)).astype(jnp.bfloat16)
    fwd_hr, fwd_hi = dft_tables(TH, -1.0)
    fwd_wr, fwd_wi = dft_tables(TW, -1.0)
    inv_hr, inv_hi = dft_tables(TH, 1.0)
    inv_wr, inv_wi = dft_tables(TW, 1.0)
    scale = 1.0 / math.sqrt(TH * TW)

    def forward_band(pair):
        band_r, band_i = pair
        rows_r, rows_i = left_apply(fwd_hr, fwd_hi, band_r, band_i)
        rows_r = rows_r.astype(jnp.bfloat16).reshape(TH, N_WIDE, TW)
        rows_i = rows_i.astype(jnp.bfloat16).reshape(TH, N_WIDE, TW)
        spec_r, spec_i = tile_right(rows_r, rows_i, fwd_wr, fwd_wi)
        return ((spec_r * scale).astype(jnp.bfloat16), (spec_i * scale).astype(jnp.bfloat16))
    spec_r, spec_i = lax.map(forward_band, (plane_r.reshape(N_NARROW, TH, NX), plane_i.reshape(N_NARROW, TH, NX)))
    pad_r = jnp.pad(spec_r, ((0, 0), (0, 0), (2, 2), (0, 0)))
    pad_i = jnp.pad(spec_i, ((0, 0), (0, 0), (2, 2), (0, 0)))
    col_r = jnp.zeros(spec_r.shape, jnp.float32)
    col_i = jnp.zeros(spec_i.shape, jnp.float32)
    for offset in range(-2, 3):
        weight = reach_weight(TW, DEPTH, float(offset))
        start = 2 - offset
        col_r = col_r + weight * pad_r[:, :, start:start + N_WIDE, :].astype(jnp.float32)
        col_i = col_i + weight * pad_i[:, :, start:start + N_WIDE, :].astype(jnp.float32)
    col_r = col_r.astype(jnp.bfloat16)
    col_i = col_i.astype(jnp.bfloat16)
    pad_r = jnp.pad(col_r, ((2, 2), (0, 0), (0, 0), (0, 0)))
    pad_i = jnp.pad(col_i, ((2, 2), (0, 0), (0, 0), (0, 0)))
    sum_r = jnp.zeros(col_r.shape, jnp.float32)
    sum_i = jnp.zeros(col_i.shape, jnp.float32)
    for offset in range(-2, 3):
        weight = reach_weight(TH, DEPTH, float(offset))[None, :, None, None]
        start = 2 - offset
        sum_r = sum_r + weight * pad_r[start:start + N_NARROW].astype(jnp.float32)
        sum_i = sum_i + weight * pad_i[start:start + N_NARROW].astype(jnp.float32)
    angle = depth_phase(TH, DEPTH)[:, None] + depth_phase(TW, DEPTH)[None, :]
    phase_r = jnp.cos(angle)[None, :, None, :]
    phase_i = jnp.sin(angle)[None, :, None, :]
    focus_r = (phase_r * sum_r - phase_i * sum_i).astype(jnp.bfloat16)
    focus_i = (phase_r * sum_i + phase_i * sum_r).astype(jnp.bfloat16)

    def inverse_band(pair):
        band_r, band_i = pair
        cols_r, cols_i = tile_right(band_r, band_i, inv_wr, inv_wi)
        cols_r = cols_r.astype(jnp.bfloat16).reshape(TH, NX)
        cols_i = cols_i.astype(jnp.bfloat16).reshape(TH, NX)
        out_r, out_i = left_apply(inv_hr, inv_hi, cols_r, cols_i)
        return (out_r * scale, out_i * scale)
    holo_r, holo_i = lax.map(inverse_band, (focus_r, focus_i))
    return jnp.stack([holo_r.reshape(NY, NX), holo_i.reshape(NY, NX)])
```

```python
import math

import jax
import jax.numpy as jnp
import numpy as np
from jax import lax
from jax.sharding import PartitionSpec as P

TH = 512
TW = 256
FACET = 16
DEPTH = 1280
REACH = 2
SPREAD = 16.0
PIXELS = FACET * FACET
WORDS = 2 * PIXELS + 128


def dft_tables(length, spin_sign):
    position = np.arange(length)
    angles = (position[:, None] * position[None, :] % length) * (2.0 * math.pi / length)
    as_bf16 = lambda v: np.asarray(v, np.float32).astype(jnp.bfloat16)
    return as_bf16(np.cos(angles)), as_bf16(spin_sign * np.sin(angles))


def signed_frequency(length):
    return (np.arange(length) + length // 2) % length - length // 2


def reach_weight(length, offset):
    travel = signed_frequency(length) * (DEPTH / (length * length))
    return np.exp(-((travel - offset) ** 2) / SPREAD).astype(np.float32)


def depth_phase(length):
    frequency = signed_frequency(length)
    return (DEPTH * frequency * frequency % (2 * length * length)) * (-math.pi / (length * length))


def render(amplitude, tilt):
    position = jnp.arange(PIXELS, dtype=jnp.int32)
    row_pos = (position // FACET).astype(jnp.float32)
    col_pos = (position % FACET).astype(jnp.float32)
    phase = (
        tilt[0][:, None] * row_pos[None, :] + tilt[1][:, None] * col_pos[None, :] + tilt[2][:, None]
    )
    return (
        (amplitude * jnp.cos(phase)).astype(jnp.bfloat16),
        (amplitude * jnp.sin(phase)).astype(jnp.bfloat16),
    )


def dot(a, b):
    return jnp.dot(a, b, preferred_element_type=jnp.float32)


def left_apply(table, pair):
    both = dot(table, pair)
    half, wide = table.shape[0] // 2, pair.shape[1] // 2
    top, low = both[:half], both[half:]
    return top[:, :wide] - low[:, wide:], top[:, wide:] + low[:, :wide]


def right_apply(pair, table):
    both = dot(pair, table)
    half, wide = pair.shape[0] // 2, table.shape[1] // 2
    top, low = both[:half], both[half:]
    return top[:, :wide] - low[:, wide:], top[:, wide:] + low[:, :wide]


def exchange(amplitude, tilt, owner, row_offset, col_offset):
    wide_count, narrow_count = lax.axis_size("wide"), lax.axis_size("narrow")
    band = lax.axis_index("narrow")
    facet_count = amplitude.shape[0]
    slot_count = max(2, (3 * facet_count + wide_count - 1) // wide_count)
    total_slots = wide_count * slot_count
    field_r, field_i = render(amplitude, tilt)
    marks = jnp.stack(
        [owner[:, 0], row_offset // 16, row_offset % 16, col_offset // 16, col_offset % 16], axis=1
    ).astype(jnp.bfloat16)
    marks = jnp.pad(marks, ((0, 0), (0, 128 - marks.shape[1])))
    packed = jnp.concatenate([field_r, field_i, marks], axis=1)
    packed = lax.all_gather(packed, "narrow", axis=0, tiled=False)
    bands = min(narrow_count, 2 * REACH + 1)
    first = jnp.clip(band - REACH, 0, narrow_count - bands)
    if bands < narrow_count:
        packed = lax.dynamic_slice_in_dim(packed, first, bands, 0)
    target = packed[:, :, 2 * PIXELS].astype(jnp.int32)
    chosen = target[:, :, None] == jnp.arange(wide_count, dtype=jnp.int32)[None, None, :]
    earlier = jnp.asarray(np.tril(np.ones((facet_count, facet_count), np.float32), -1), jnp.bfloat16)
    rank = jnp.einsum(
        "fg,bgc->bfc", earlier, chosen.astype(jnp.bfloat16), preferred_element_type=jnp.float32
    )
    rank = jnp.sum(jnp.where(chosen, rank, 0.0), axis=2).astype(jnp.int32)
    slot_at = target * slot_count + rank
    pick = slot_at[:, None, :] == jnp.arange(total_slots, dtype=jnp.int32)[None, :, None]
    outgoing = jnp.einsum(
        "bsf,bfp->bsp", pick.astype(jnp.bfloat16), packed, preferred_element_type=jnp.float32
    ).astype(jnp.bfloat16)
    incoming = lax.all_to_all(
        outgoing.reshape(bands, wide_count, slot_count, WORDS),
        "wide",
        split_axis=1,
        concat_axis=1,
        tiled=True,
    )
    return incoming.reshape(bands, total_slots, WORDS), band - first


def place(incoming):
    bands, total_slots, _ = incoming.shape
    fields = incoming[:, :, : 2 * PIXELS].reshape(bands, total_slots, 2, FACET, FACET)
    marks = incoming[:, :, 2 * PIXELS : 2 * PIXELS + 8].astype(jnp.int32)
    row_at = marks[:, :, 1] * 16 + marks[:, :, 2]
    col_at = marks[:, :, 3] * 16 + marks[:, :, 4]
    pixel = jnp.arange(FACET, dtype=jnp.int32)
    col_hot = (
        jnp.arange(TW, dtype=jnp.int32) == col_at[:, :, None, None] + pixel[:, None]
    ).astype(jnp.bfloat16)
    spread = jnp.einsum(
        "bscuv,bsvx->bsucx", fields, col_hot, preferred_element_type=jnp.float32
    ).astype(jnp.bfloat16)
    row_hot = (
        jnp.arange(TH, dtype=jnp.int32)[:, None, None] == row_at[:, None, :, None] + pixel
    ).astype(jnp.bfloat16)
    plane = jnp.einsum(
        "byk,bkx->byx",
        row_hot.reshape(bands, TH, total_slots * FACET),
        spread.reshape(bands, total_slots * FACET, 2 * TW),
        preferred_element_type=jnp.float32,
    )
    return plane.astype(jnp.bfloat16)


def local(amplitude, tilt, owner, row_offset, col_offset):
    wide_count = lax.axis_size("wide")
    column = lax.axis_index("wide")
    incoming, here = exchange(amplitude, tilt, owner, row_offset, col_offset)
    plane = place(incoming)
    bands = plane.shape[0]
    scale = 1.0 / math.sqrt(TH * TW)

    most = bands - 1
    by_offset = np.zeros((2 * most + 1, TH), np.float32)
    for offset in range(-REACH, REACH + 1):
        if abs(offset) <= most:
            by_offset[offset + most] = reach_weight(TH, float(offset))
    weights = lax.dynamic_slice_in_dim(jnp.asarray(by_offset[::-1].copy()), most - here, bands, 0)
    fwd_hr, fwd_hi = dft_tables(TH, -1.0)
    fwd_h = jnp.asarray(np.concatenate([fwd_hr, fwd_hi], axis=0))
    row_w = jnp.concatenate([weights, weights], axis=1)
    tables = (row_w[:, :, None] * fwd_h[None].astype(jnp.float32)).astype(jnp.bfloat16)
    tables = jnp.transpose(tables, (1, 0, 2)).reshape(2 * TH, bands * TH)
    rows_r, rows_i = left_apply(tables, plane.reshape(bands * TH, 2 * TW))
    fwd_w = jnp.asarray(np.concatenate(dft_tables(TW, -1.0), axis=1))
    pair = jnp.concatenate([rows_r, rows_i], axis=0).astype(jnp.bfloat16)
    spec_r, spec_i = right_apply(pair, fwd_w)
    spectrum = (jnp.stack([spec_r, spec_i]) * scale).astype(jnp.bfloat16)

    rows = TH // wide_count
    parts = lax.all_to_all(
        spectrum.reshape(2, wide_count, rows, TW), "wide", split_axis=1, concat_axis=1, tiled=True
    )
    padded = jnp.pad(parts.astype(jnp.float32), ((0, 0), (REACH, REACH), (0, 0), (0, 0)))
    total = 0.0
    for offset in range(-REACH, REACH + 1):
        start = REACH - offset
        total = total + jnp.asarray(reach_weight(TW, float(offset))) * padded[
            :, start : start + wide_count
        ]
    angle = depth_phase(TH)[:, None] + depth_phase(TW)[None, :]
    phase_r = lax.dynamic_slice_in_dim(
        jnp.asarray(np.cos(angle).astype(np.float32)), column * rows, rows, 0
    )
    phase_i = lax.dynamic_slice_in_dim(
        jnp.asarray(np.sin(angle).astype(np.float32)), column * rows, rows, 0
    )
    focus = jnp.stack(
        [phase_r * total[0] - phase_i * total[1], phase_r * total[1] + phase_i * total[0]]
    ).astype(jnp.bfloat16)
    focus = lax.all_to_all(focus, "wide", split_axis=1, concat_axis=1, tiled=True)
    inv_w = jnp.asarray(np.concatenate(dft_tables(TW, 1.0), axis=1))
    inv_h = jnp.asarray(np.concatenate(dft_tables(TH, 1.0), axis=0))
    cols_r, cols_i = right_apply(focus.reshape(2 * TH, TW), inv_w)
    pair = jnp.concatenate([cols_r, cols_i], axis=1).astype(jnp.bfloat16)
    out_r, out_i = left_apply(inv_h, pair)
    return jnp.stack([out_r, out_i]) * scale


def solution(mesh):
    in_specs = (
        P(("wide", "narrow"), None),
        P(None, ("wide", "narrow")),
        P(("wide", "narrow"), None),
        P(("wide", "narrow")),
        P(("wide", "narrow")),
    )
    out_specs = P(None, "narrow", "wide")
    return jax.shard_map(local, mesh=mesh, in_specs=in_specs, out_specs=out_specs, check_vma=False)
```

```python
import functools
import math

import jax
import jax.numpy as jnp
import numpy as np
from jax import lax
from jax.experimental import pallas as pl
from jax.experimental.pallas import tpu as pltpu
from jax.sharding import PartitionSpec as P

TH = 512
TW = 256
FACET = 16
DEPTH = 1280
REACH = 2
SPREAD = 16.0
PIXELS = FACET * FACET
WORDS = 2 * PIXELS + 128


def dft_tables(length, spin_sign):
    position = np.arange(length)
    angles = (position[:, None] * position[None, :] % length) * (2.0 * math.pi / length)
    as_bf16 = lambda v: np.asarray(v, np.float32).astype(jnp.bfloat16)
    return as_bf16(np.cos(angles)), as_bf16(spin_sign * np.sin(angles))


def signed_frequency(length):
    return (np.arange(length) + length // 2) % length - length // 2


def reach_weight(length, offset):
    travel = signed_frequency(length) * (DEPTH / (length * length))
    return np.exp(-((travel - offset) ** 2) / SPREAD).astype(np.float32)


def depth_phase(length):
    frequency = signed_frequency(length)
    return (DEPTH * frequency * frequency % (2 * length * length)) * (-math.pi / (length * length))


def render_kernel(amp_ref, par_ref, out_ref):
    par = par_ref[...]
    tilt_r, tilt_c, lead = par[:, 0:1], par[:, 1:2], par[:, 2:3]
    owner, row_at, col_at = par[:, 3:4], par[:, 4:5], par[:, 5:6]
    lane = lax.broadcasted_iota(jnp.int32, amp_ref.shape, 1)
    across = lane % FACET
    col_hi = jnp.floor(col_at * (1.0 / FACET))
    col_lo = col_at - FACET * col_hi
    row_hi = jnp.floor(row_at * (1.0 / FACET))
    row_lo = row_at - FACET * row_hi
    turn = col_lo.astype(jnp.int32)
    amp = amp_ref[...]
    for step in (1, 2, 4, 8):
        near = pltpu.roll(amp, step, 1)
        far = pltpu.roll(amp, PIXELS + step - FACET, 1)
        turned = jnp.where(across >= step, near, far)
        amp = jnp.where((turn & step) != 0, turned, amp)
    pixel = ((across - turn) & (FACET - 1)).astype(jnp.float32)
    phase = tilt_r * (lane // FACET).astype(jnp.float32) + tilt_c * pixel + lead
    real, imag = (amp * jnp.cos(phase)).astype(jnp.bfloat16), (amp * jnp.sin(phase)).astype(jnp.bfloat16)
    half = PIXELS // 2
    out_ref[:, 0:half] = real[:, :half]
    out_ref[:, half : 2 * half] = imag[:, :half]
    out_ref[:, 2 * half : 3 * half] = real[:, half:]
    out_ref[:, 3 * half : 4 * half] = imag[:, half:]
    spot = lax.broadcasted_iota(jnp.int32, (amp.shape[0], 128), 1)
    marks = jnp.where(spot == 0, owner, 0.0)
    for at, value in ((1, row_hi), (2, row_lo), (3, col_hi), (4, col_lo)):
        marks = jnp.where(spot == at, value, marks)
    out_ref[:, 4 * half :] = marks.astype(jnp.bfloat16)


def render(amplitude, tilt, owner, row_offset, col_offset):
    par = jnp.concatenate(
        [tilt, jnp.stack([owner[:, 0], row_offset, col_offset]).astype(jnp.float32)], axis=0
    )
    par = jnp.pad(par.T, ((0, 0), (0, 2)))
    return pl.pallas_call(
        render_kernel,
        out_shape=jax.ShapeDtypeStruct((amplitude.shape[0], WORDS), jnp.bfloat16),
    )(amplitude, par)


def dot(a, b):
    return jnp.dot(a, b, preferred_element_type=jnp.float32)


def left_apply(table, pair):
    both = dot(table, pair)
    half, wide = table.shape[0] // 2, pair.shape[1] // 2
    top, low = both[:half], both[half:]
    return top[:, :wide] - low[:, wide:], top[:, wide:] + low[:, :wide]


def right_apply(pair, table):
    both = dot(pair, table)
    half, wide = pair.shape[0] // 2, table.shape[1] // 2
    top, low = both[:half], both[half:]
    return top[:, :wide] - low[:, wide:], top[:, wide:] + low[:, :wide]


def exchange(amplitude, tilt, owner, row_offset, col_offset):
    wide_count, narrow_count = lax.axis_size("wide"), lax.axis_size("narrow")
    band = lax.axis_index("narrow")
    facet_count = amplitude.shape[0]
    slot_count = max(2, (3 * facet_count + wide_count - 1) // wide_count)
    total_slots = wide_count * slot_count
    packed = render(amplitude, tilt, owner, row_offset, col_offset)
    packed = lax.all_gather(packed, "narrow", axis=0, tiled=False)
    bands = min(narrow_count, 2 * REACH + 1)
    first = jnp.clip(band - REACH, 0, narrow_count - bands)
    if bands < narrow_count:
        packed = lax.dynamic_slice_in_dim(packed, first, bands, 0)
    target = packed[:, :, 2 * PIXELS].astype(jnp.int32)
    chosen = target[:, :, None] == jnp.arange(wide_count, dtype=jnp.int32)[None, None, :]
    earlier = jnp.asarray(np.tril(np.ones((facet_count, facet_count), np.float32), -1), jnp.bfloat16)
    rank = jnp.einsum(
        "fg,bgc->bfc", earlier, chosen.astype(jnp.bfloat16), preferred_element_type=jnp.float32
    )
    rank = jnp.sum(jnp.where(chosen, rank, 0.0), axis=2).astype(jnp.int32)
    slot_at = target * slot_count + rank
    pick = slot_at[:, None, :] == jnp.arange(total_slots, dtype=jnp.int32)[None, :, None]
    outgoing = jnp.einsum(
        "bsf,bfp->bsp", pick.astype(jnp.bfloat16), packed, preferred_element_type=jnp.float32
    ).astype(jnp.bfloat16)
    incoming = lax.all_to_all(
        outgoing.reshape(bands, wide_count, slot_count, WORDS),
        "wide",
        split_axis=1,
        concat_axis=1,
        tiled=True,
    )
    return incoming.reshape(bands, total_slots, WORDS), band - first


def forward_kernel(bands, slots, pay_ref, tile_ref, tab_ref, wide_ref, out_ref, mask, spread, plane, total):
    half = PIXELS
    marks = pay_ref[:, 2 * PIXELS :].astype(jnp.float32)
    col_at = FACET * marks[:, 3:4] + marks[:, 4:5]
    spot = (lax.broadcasted_iota(jnp.int32, mask.shape, 1) % TW).astype(jnp.float32) - col_at
    mask[...] = jnp.where((spot >= 0.0) & (spot < FACET), 1.0, 0.0)
    for side in range(2):
        fields = pay_ref[:, side * half : (side + 1) * half]

        def widen(at, _):
            pixels = dot(fields, tile_ref[at]) * mask[...]
            pixels = pixels.astype(jnp.bfloat16)
            row = pl.multiple_of((side * (FACET // 2) + at) * slots, slots)
            for b in range(bands):
                spread[b, pl.ds(row, slots), :] = pixels[b * slots : (b + 1) * slots]
            return 0

        lax.fori_loop(0, FACET // 2, widen, 0)
    lane = lax.broadcasted_iota(jnp.int32, (8, 128), 1)
    select = jnp.where(lane == 1, float(FACET), jnp.where(lane == 2, 1.0, 0.0)).astype(jnp.bfloat16)
    group = 4
    depth = group * slots
    spot = lax.broadcasted_iota(jnp.int32, (TH, depth), 0).astype(jnp.float32)
    for b in range(bands):
        corner = pay_ref[b * slots : (b + 1) * slots, 2 * PIXELS :]
        row_at = lax.dot_general(
            select, corner, (((1,), (1,)), ((), ())), preferred_element_type=jnp.float32
        )[0:1]
        row_at = jnp.concatenate([row_at + float(u) for u in range(group)], axis=1)
        plane[...] = jnp.zeros_like(plane)

        def add_rows(at, _):
            step = (at * group).astype(jnp.float32)
            hot = jnp.where(spot == row_at + step, 1.0, 0.0).astype(jnp.bfloat16)
            plane[...] += dot(hot, spread[b, pl.ds(pl.multiple_of(at * depth, depth), depth), :])
            return 0

        lax.fori_loop(0, FACET // group, add_rows, 0)
        rows = dot(tab_ref[:, b * TH : (b + 1) * TH], plane[...].astype(jnp.bfloat16))
        total[...] = rows if b == 0 else total[...] + rows
    scale = 1.0 / math.sqrt(TH * TW)
    real = (total[:TH, :TW] - total[TH:, TW:]).astype(jnp.bfloat16)
    imag = (total[:TH, TW:] + total[TH:, :TW]).astype(jnp.bfloat16)
    by_real, by_imag = dot(real, wide_ref[...]), dot(imag, wide_ref[...])
    out_ref[0] = ((by_real[:, :TW] - by_imag[:, TW:]) * scale).astype(jnp.bfloat16)
    out_ref[1] = ((by_real[:, TW:] + by_imag[:, :TW]) * scale).astype(jnp.bfloat16)


def tile_tables():
    lane = np.arange(PIXELS)[None, :, None]
    spot = np.arange(2 * TW)[None, None, :]
    at = np.arange(FACET // 2)[:, None, None]
    same = (lane // 128 == spot // TW) & (lane % 128 == at * FACET + spot % FACET)
    return same.astype(np.float32).astype(jnp.bfloat16)


def forward(incoming, tables, fwd_w):
    bands, slots, _ = incoming.shape
    return pl.pallas_call(
        functools.partial(forward_kernel, bands, slots),
        out_shape=jax.ShapeDtypeStruct((2, TH, TW), jnp.bfloat16),
        scratch_shapes=[
            pltpu.VMEM((bands * slots, 2 * TW), jnp.float32),
            pltpu.VMEM((bands, FACET * slots, 2 * TW), jnp.bfloat16),
            pltpu.VMEM((TH, 2 * TW), jnp.float32),
            pltpu.VMEM((2 * TH, 2 * TW), jnp.float32),
        ],
        compiler_params=pltpu.CompilerParams(vmem_limit_bytes=48 * 2**20),
    )(incoming.reshape(bands * slots, WORDS), jnp.asarray(tile_tables()), tables, fwd_w)


def local(amplitude, tilt, owner, row_offset, col_offset):
    wide_count = lax.axis_size("wide")
    column = lax.axis_index("wide")
    incoming, here = exchange(amplitude, tilt, owner, row_offset, col_offset)
    bands = incoming.shape[0]
    scale = 1.0 / math.sqrt(TH * TW)

    most = bands - 1
    by_offset = np.zeros((2 * most + 1, TH), np.float32)
    for offset in range(-REACH, REACH + 1):
        if abs(offset) <= most:
            by_offset[offset + most] = reach_weight(TH, float(offset))
    weights = lax.dynamic_slice_in_dim(jnp.asarray(by_offset[::-1].copy()), most - here, bands, 0)
    fwd_hr, fwd_hi = dft_tables(TH, -1.0)
    fwd_h = jnp.asarray(np.concatenate([fwd_hr, fwd_hi], axis=0))
    row_w = jnp.concatenate([weights, weights], axis=1)
    tables = (row_w[:, :, None] * fwd_h[None].astype(jnp.float32)).astype(jnp.bfloat16)
    tables = jnp.transpose(tables, (1, 0, 2)).reshape(2 * TH, bands * TH)
    fwd_w = jnp.asarray(np.concatenate(dft_tables(TW, -1.0), axis=1))
    spectrum = forward(incoming, tables, fwd_w)

    rows = TH // wide_count
    parts = lax.all_to_all(
        spectrum.reshape(2, wide_count, rows, TW), "wide", split_axis=1, concat_axis=1, tiled=True
    )
    padded = jnp.pad(parts.astype(jnp.float32), ((0, 0), (REACH, REACH), (0, 0), (0, 0)))
    total = 0.0
    for offset in range(-REACH, REACH + 1):
        start = REACH - offset
        total = total + jnp.asarray(reach_weight(TW, float(offset))) * padded[
            :, start : start + wide_count
        ]
    angle = depth_phase(TH)[:, None] + depth_phase(TW)[None, :]
    phase_r = lax.dynamic_slice_in_dim(
        jnp.asarray(np.cos(angle).astype(np.float32)), column * rows, rows, 0
    )
    phase_i = lax.dynamic_slice_in_dim(
        jnp.asarray(np.sin(angle).astype(np.float32)), column * rows, rows, 0
    )
    focus = jnp.stack(
        [phase_r * total[0] - phase_i * total[1], phase_r * total[1] + phase_i * total[0]]
    ).astype(jnp.bfloat16)
    focus = lax.all_to_all(focus, "wide", split_axis=1, concat_axis=1, tiled=True)
    inv_w = jnp.asarray(np.concatenate(dft_tables(TW, 1.0), axis=1))
    inv_h = jnp.asarray(np.concatenate(dft_tables(TH, 1.0), axis=0))
    cols_r, cols_i = right_apply(focus.reshape(2 * TH, TW), inv_w)
    pair = jnp.concatenate([cols_r, cols_i], axis=1).astype(jnp.bfloat16)
    out_r, out_i = left_apply(inv_h, pair)
    return jnp.stack([out_r, out_i]) * scale


def solution(mesh):
    in_specs = (
        P(("wide", "narrow"), None),
        P(None, ("wide", "narrow")),
        P(("wide", "narrow"), None),
        P(("wide", "narrow")),
        P(("wide", "narrow")),
    )
    out_specs = P(None, "narrow", "wide")
    return jax.shard_map(local, mesh=mesh, in_specs=in_specs, out_specs=out_specs, check_vma=False)
```

```python
import functools
import math

import jax
import jax.numpy as jnp
import numpy as np
from jax import lax
from jax.experimental import pallas as pl
from jax.experimental.pallas import tpu as pltpu
from jax.sharding import PartitionSpec as P

TH = 512
TW = 256
FACET = 16
DEPTH = 1280
REACH = 2
SPREAD = 16.0
PIXELS = FACET * FACET
WORDS = 2 * PIXELS + 128


def dft_tables(length, spin_sign):
    position = np.arange(length)
    angles = (position[:, None] * position[None, :] % length) * (2.0 * math.pi / length)
    as_bf16 = lambda v: np.asarray(v, np.float32).astype(jnp.bfloat16)
    return as_bf16(np.cos(angles)), as_bf16(spin_sign * np.sin(angles))


def signed_frequency(length):
    return (np.arange(length) + length // 2) % length - length // 2


def reach_weight(length, offset):
    travel = signed_frequency(length) * (DEPTH / (length * length))
    return np.exp(-((travel - offset) ** 2) / SPREAD).astype(np.float32)


def depth_phase(length):
    frequency = signed_frequency(length)
    return (DEPTH * frequency * frequency % (2 * length * length)) * (-math.pi / (length * length))


def render_into(amp_ref, par_ref, out_ref):
    par = par_ref[...]
    tilt_r, tilt_c, lead = par[:, 0:1], par[:, 1:2], par[:, 2:3]
    owner, row_at, col_at = par[:, 3:4], par[:, 4:5], par[:, 5:6]
    lane = lax.broadcasted_iota(jnp.int32, amp_ref.shape, 1)
    across = lane % FACET
    col_hi = jnp.floor(col_at * (1.0 / FACET))
    col_lo = col_at - FACET * col_hi
    row_hi = jnp.floor(row_at * (1.0 / FACET))
    row_lo = row_at - FACET * row_hi
    turn = col_lo.astype(jnp.int32)
    amp = amp_ref[...]
    for step in (1, 2, 4, 8):
        near = pltpu.roll(amp, step, 1)
        far = pltpu.roll(amp, PIXELS + step - FACET, 1)
        turned = jnp.where(across >= step, near, far)
        amp = jnp.where((turn & step) != 0, turned, amp)
    pixel = ((across - turn) & (FACET - 1)).astype(jnp.float32)
    phase = tilt_r * (lane // FACET).astype(jnp.float32) + tilt_c * pixel + lead
    real, imag = (amp * jnp.cos(phase)).astype(jnp.bfloat16), (amp * jnp.sin(phase)).astype(jnp.bfloat16)
    half = PIXELS // 2
    out_ref[:, 0:half] = real[:, :half]
    out_ref[:, half : 2 * half] = imag[:, :half]
    out_ref[:, 2 * half : 3 * half] = real[:, half:]
    out_ref[:, 3 * half : 4 * half] = imag[:, half:]
    spot = lax.broadcasted_iota(jnp.int32, (amp.shape[0], 128), 1)
    marks = jnp.where(spot == 0, owner, 0.0)
    for at, value in ((1, row_hi), (2, row_lo), (3, col_hi), (4, col_lo)):
        marks = jnp.where(spot == at, value, marks)
    out_ref[:, 4 * half :] = marks.astype(jnp.bfloat16)


MESH = pl.DeviceIdType.MESH


def greet(targets):
    barrier = pltpu.get_barrier_semaphore()
    for valid, target in targets:
        if valid is True:
            pl.semaphore_signal(barrier, inc=1, device_id=target, device_id_type=MESH)
        else:

            @pl.when(valid)
            def _():
                pl.semaphore_signal(barrier, inc=1, device_id=target, device_id_type=MESH)

    count = 0
    for valid, _ in targets:
        count = count + (1 if valid is True else valid.astype(jnp.int32))
    pl.semaphore_wait(barrier, count)


def front_kernel(
    wide, narrow, bands, per, amp_ref, par_ref, out_ref, gathered, outgoing, incoming, send_n, recv_n, send_w, recv_w
):
    column, band = lax.axis_index("wide"), lax.axis_index("narrow")
    block = outgoing.shape[1]

    def first_of(where):
        return jnp.clip(where - REACH, 0, narrow - bands)

    first = first_of(band)
    deltas = [d for d in range(-REACH, REACH + 1) if d != 0]
    targets = [((band + d >= 0) & (band + d < narrow), (column, band + d)) for d in deltas]
    peers = [(True, (lax.rem(column + step, wide), band)) for step in range(1, wide)]
    greet(targets + peers)
    render_into(amp_ref, par_ref, gathered.at[band - first])

    def narrow_copy(k):
        there = jnp.clip(band + deltas[k], 0, narrow - 1)
        return pltpu.make_async_remote_copy(
            src_ref=gathered.at[band - first],
            dst_ref=gathered.at[jnp.clip(band - first_of(there), 0, bands - 1)],
            send_sem=send_n.at[k],
            recv_sem=recv_n.at[k],
            device_id=(column, there),
            device_id_type=MESH,
        )

    for k in range(len(deltas)):

        @pl.when(targets[k][0])
        def _(k=k):
            narrow_copy(k).start()

    for i in range(bands):
        away = first + i - band

        @pl.when((away > REACH) | (away < -REACH))
        def _(i=i):
            gathered[i] = jnp.zeros(gathered.shape[1:], gathered.dtype)

    for k, d in enumerate(deltas):

        @pl.when((band - d >= 0) & (band - d < narrow))
        def _(k=k):
            narrow_copy(k).wait_recv()

    facets = amp_ref.shape[0]
    lane = lax.broadcasted_iota(jnp.int32, (facets, 128), 1)
    below = lax.broadcasted_iota(jnp.int32, (facets, facets), 0) > lax.broadcasted_iota(
        jnp.int32, (facets, facets), 1
    )
    earlier = jnp.where(below, 1.0, 0.0).astype(jnp.bfloat16)
    select = jnp.where(lax.broadcasted_iota(jnp.int32, (8, 128), 1) == 0, 1.0, 0.0).astype(jnp.bfloat16)
    spot = lax.broadcasted_iota(jnp.int32, (wide * per, facets), 0).astype(jnp.float32)
    sorted_by_owner = []
    for i in range(bands):
        packed = gathered[i]
        owner = packed[:, 2 * PIXELS :].astype(jnp.float32)[:, 0:1]
        chosen = jnp.where(lane.astype(jnp.float32) == owner, 1.0, 0.0)
        rank = jnp.sum(dot(earlier, chosen.astype(jnp.bfloat16)) * chosen, axis=1, keepdims=True)
        slot = jnp.where(lane == 0, owner * float(per) + rank, 0.0).astype(jnp.bfloat16)
        slot = lax.dot_general(
            select, slot, (((1,), (1,)), ((), ())), preferred_element_type=jnp.float32
        )[0:1]
        pick = jnp.where(spot == slot, 1.0, 0.0).astype(jnp.bfloat16)
        sorted_by_owner.append(dot(pick, packed))
    spare = block - bands * per
    for w in range(wide):
        pieces = [one[w * per : (w + 1) * per] for one in sorted_by_owner]
        if spare:
            pieces.append(jnp.zeros((spare, WORDS), jnp.float32))
        outgoing[w] = jnp.concatenate(pieces, axis=0).astype(jnp.bfloat16)

    def wide_copy(step):
        there = lax.rem(column + step, wide)
        return pltpu.make_async_remote_copy(
            src_ref=outgoing.at[there],
            dst_ref=incoming.at[column],
            send_sem=send_w.at[step],
            recv_sem=recv_w.at[step],
            device_id=(there, band),
            device_id_type=MESH,
        )

    for step in range(1, wide):
        wide_copy(step).start()
    incoming[column] = outgoing[column]
    for step in range(1, wide):
        wide_copy(step).wait_recv()
    blocks = [incoming[w].astype(jnp.float32) for w in range(wide)]
    for i in range(bands):
        rows = jnp.concatenate([one[i * per : (i + 1) * per] for one in blocks], axis=0)
        out_ref[i * wide * per : (i + 1) * wide * per, :] = rows.astype(jnp.bfloat16)
    for step in range(1, wide):
        wide_copy(step).wait_send()
    for k in range(len(deltas)):

        @pl.when(targets[k][0])
        def _(k=k):
            narrow_copy(k).wait_send()


def exchange(amplitude, tilt, owner, row_offset, col_offset):
    wide, narrow = lax.axis_size("wide"), lax.axis_size("narrow")
    band = lax.axis_index("narrow")
    facets = amplitude.shape[0]
    per = max(2, (3 * facets + wide - 1) // wide)
    bands = min(narrow, 2 * REACH + 1)
    block = (bands * per + 15) // 16 * 16
    par = jnp.concatenate(
        [tilt, jnp.stack([owner[:, 0], row_offset, col_offset]).astype(jnp.float32)], axis=0
    )
    par = jnp.pad(par.T, ((0, 0), (0, 2)))
    incoming = pl.pallas_call(
        functools.partial(front_kernel, wide, narrow, bands, per),
        out_shape=jax.ShapeDtypeStruct((bands * wide * per, WORDS), jnp.bfloat16),
        in_specs=[pl.BlockSpec(memory_space=pltpu.VMEM)] * 2,
        out_specs=pl.BlockSpec(memory_space=pltpu.VMEM),
        scratch_shapes=[
            pltpu.VMEM((bands, facets, WORDS), jnp.bfloat16),
            pltpu.VMEM((wide, block, WORDS), jnp.bfloat16),
            pltpu.VMEM((wide, block, WORDS), jnp.bfloat16),
            pltpu.SemaphoreType.DMA((2 * REACH,)),
            pltpu.SemaphoreType.DMA((2 * REACH,)),
            pltpu.SemaphoreType.DMA((wide,)),
            pltpu.SemaphoreType.DMA((wide,)),
        ],
        compiler_params=pltpu.CompilerParams(
            collective_id=0, has_side_effects=True, vmem_limit_bytes=32 * 2**20
        ),
    )(amplitude, par)
    first = jnp.clip(band - REACH, 0, narrow - bands)
    return incoming.reshape(bands, wide * per, WORDS), band - first


def dot(a, b):
    return jnp.dot(a, b, preferred_element_type=jnp.float32)


def forward_kernel(bands, slots, pay_ref, tile_ref, tab_ref, wide_ref, out_ref, mask, spread, plane, total):
    half = PIXELS
    marks = pay_ref[:, 2 * PIXELS :].astype(jnp.float32)
    col_at = FACET * marks[:, 3:4] + marks[:, 4:5]
    spot = (lax.broadcasted_iota(jnp.int32, mask.shape, 1) % TW).astype(jnp.float32) - col_at
    mask[...] = jnp.where((spot >= 0.0) & (spot < FACET), 1.0, 0.0)
    for side in range(2):
        fields = pay_ref[:, side * half : (side + 1) * half]

        def widen(at, _):
            pixels = dot(fields, tile_ref[at]) * mask[...]
            pixels = pixels.astype(jnp.bfloat16)
            row = pl.multiple_of((side * (FACET // 2) + at) * slots, slots)
            for b in range(bands):
                spread[b, pl.ds(row, slots), :] = pixels[b * slots : (b + 1) * slots]
            return 0

        lax.fori_loop(0, FACET // 2, widen, 0)
    lane = lax.broadcasted_iota(jnp.int32, (8, 128), 1)
    select = jnp.where(lane == 1, float(FACET), jnp.where(lane == 2, 1.0, 0.0)).astype(jnp.bfloat16)
    group = 4
    depth = group * slots
    spot = lax.broadcasted_iota(jnp.int32, (TH, depth), 0).astype(jnp.float32)
    for b in range(bands):
        corner = pay_ref[b * slots : (b + 1) * slots, 2 * PIXELS :]
        row_at = lax.dot_general(
            select, corner, (((1,), (1,)), ((), ())), preferred_element_type=jnp.float32
        )[0:1]
        row_at = jnp.concatenate([row_at + float(u) for u in range(group)], axis=1)
        plane[...] = jnp.zeros_like(plane)

        def add_rows(at, _):
            step = (at * group).astype(jnp.float32)
            hot = jnp.where(spot == row_at + step, 1.0, 0.0).astype(jnp.bfloat16)
            plane[...] += dot(hot, spread[b, pl.ds(pl.multiple_of(at * depth, depth), depth), :])
            return 0

        lax.fori_loop(0, FACET // group, add_rows, 0)
        rows = dot(tab_ref[:, b * TH : (b + 1) * TH], plane[...].astype(jnp.bfloat16))
        total[...] = rows if b == 0 else total[...] + rows
    scale = 1.0 / math.sqrt(TH * TW)
    real = (total[:TH, :TW] - total[TH:, TW:]).astype(jnp.bfloat16)
    imag = (total[:TH, TW:] + total[TH:, :TW]).astype(jnp.bfloat16)
    by_real, by_imag = dot(real, wide_ref[...]), dot(imag, wide_ref[...])
    spec_r = (by_real[:, :TW] - by_imag[:, TW:]) * scale
    spec_i = (by_real[:, TW:] + by_imag[:, :TW]) * scale
    wide, rows = out_ref.shape[0], out_ref.shape[1] // 2
    for w in range(wide):
        here = slice(w * rows, (w + 1) * rows)
        out_ref[w] = jnp.concatenate([spec_r[here], spec_i[here]], axis=0).astype(jnp.bfloat16)


def tile_tables():
    lane = np.arange(PIXELS)[None, :, None]
    spot = np.arange(2 * TW)[None, None, :]
    at = np.arange(FACET // 2)[:, None, None]
    same = (lane // 128 == spot // TW) & (lane % 128 == at * FACET + spot % FACET)
    return same.astype(np.float32).astype(jnp.bfloat16)


def forward(incoming, tables, fwd_w, wide):
    bands, slots, _ = incoming.shape
    return pl.pallas_call(
        functools.partial(forward_kernel, bands, slots),
        out_shape=jax.ShapeDtypeStruct((wide, 2 * TH // wide, TW), jnp.bfloat16),
        scratch_shapes=[
            pltpu.VMEM((bands * slots, 2 * TW), jnp.float32),
            pltpu.VMEM((bands, FACET * slots, 2 * TW), jnp.bfloat16),
            pltpu.VMEM((TH, 2 * TW), jnp.float32),
            pltpu.VMEM((2 * TH, 2 * TW), jnp.float32),
        ],
        compiler_params=pltpu.CompilerParams(vmem_limit_bytes=48 * 2**20),
    )(incoming.reshape(bands * slots, WORDS), jnp.asarray(tile_tables()), tables, fwd_w)


def back_kernel(
    wide, spec_ref, weight_ref, phase_r_ref, phase_i_ref, wide_ref, high_ref, out_ref,
    parts, focus, back, image, send_a, recv_a, send_b, recv_b,
):
    column, band = lax.axis_index("wide"), lax.axis_index("narrow")
    rows = TH // wide
    greet([(True, (lax.rem(column + step, wide), band)) for step in range(1, wide)])

    def copy(step, source, landing, send, recv):
        there = lax.rem(column + step, wide)
        return pltpu.make_async_remote_copy(
            src_ref=source.at[there],
            dst_ref=landing.at[column],
            send_sem=send.at[step],
            recv_sem=recv.at[step],
            device_id=(there, band),
            device_id_type=MESH,
        )

    def out_copy(step):
        return copy(step, spec_ref, parts, send_a, recv_a)

    def home_copy(step):
        return copy(step, focus, back, send_b, recv_b)

    for step in range(1, wide):
        out_copy(step).start()
    parts[column] = spec_ref[column]
    here = pl.ds(pl.multiple_of(column * rows, rows), rows)
    phase_r, phase_i = phase_r_ref[here, :], phase_i_ref[here, :]
    for step in range(1, wide):
        out_copy(step).wait_recv()
    for step in list(range(1, wide)) + [0]:
        there = lax.rem(column + step, wide)
        total = None
        for offset in range(-REACH, REACH + 1):
            source = there - offset
            inside = jnp.where((source >= 0) & (source < wide), 1.0, 0.0)
            weight = weight_ref[offset + REACH : offset + REACH + 1, :] * inside
            term = weight * parts[jnp.clip(source, 0, wide - 1)].astype(jnp.float32)
            total = term if total is None else total + term
        real, imag = total[:rows], total[rows:]
        turned = jnp.concatenate(
            [phase_r * real - phase_i * imag, phase_r * imag + phase_i * real], axis=0
        ).astype(jnp.bfloat16)
        if step:
            focus[there] = turned
            home_copy(step).start()
        else:
            back[column] = turned
    for step in range(wide):
        source = lax.rem(column - step + wide, wide)
        if step:
            home_copy(step).wait_recv()
        both = dot(back[source], wide_ref[...])
        top, low = both[:rows], both[rows:]
        image[source, :, :TW] = top[:, :TW] - low[:, TW:]
        image[source, :, TW:] = top[:, TW:] + low[:, :TW]
    scale = 1.0 / math.sqrt(TH * TW)
    pair = image[...].reshape(TH, 2 * TW).astype(jnp.bfloat16)
    top, low = dot(high_ref[:TH], pair), dot(high_ref[TH:], pair)
    out_ref[0] = (top[:, :TW] - low[:, TW:]) * scale
    out_ref[1] = (top[:, TW:] + low[:, :TW]) * scale
    for step in range(1, wide):
        out_copy(step).wait_send()
        home_copy(step).wait_send()


def backward(spectrum):
    wide = spectrum.shape[0]
    weight = np.zeros((8, TW), np.float32)
    for offset in range(-REACH, REACH + 1):
        weight[offset + REACH] = reach_weight(TW, float(offset))
    angle = depth_phase(TH)[:, None] + depth_phase(TW)[None, :]
    inv_w = np.concatenate(dft_tables(TW, 1.0), axis=1)
    inv_h = np.concatenate(dft_tables(TH, 1.0), axis=0)
    constants = [weight, np.cos(angle).astype(np.float32), np.sin(angle).astype(np.float32), inv_w, inv_h]
    piece = pltpu.VMEM(spectrum.shape, jnp.bfloat16)
    return pl.pallas_call(
        functools.partial(back_kernel, wide),
        out_shape=jax.ShapeDtypeStruct((2, TH, TW), jnp.float32),
        in_specs=[pl.BlockSpec(memory_space=pltpu.VMEM)] * 6,
        out_specs=pl.BlockSpec(memory_space=pltpu.VMEM),
        scratch_shapes=[piece, piece, piece, pltpu.VMEM((wide, TH // wide, 2 * TW), jnp.float32)]
        + [pltpu.SemaphoreType.DMA((wide,))] * 4,
        compiler_params=pltpu.CompilerParams(
            collective_id=1, has_side_effects=True, vmem_limit_bytes=32 * 2**20
        ),
    )(spectrum, *[jnp.asarray(one) for one in constants])


def local(amplitude, tilt, owner, row_offset, col_offset):
    wide_count = lax.axis_size("wide")
    incoming, here = exchange(amplitude, tilt, owner, row_offset, col_offset)
    bands = incoming.shape[0]

    most = bands - 1
    by_offset = np.zeros((2 * most + 1, TH), np.float32)
    for offset in range(-REACH, REACH + 1):
        if abs(offset) <= most:
            by_offset[offset + most] = reach_weight(TH, float(offset))
    weights = lax.dynamic_slice_in_dim(jnp.asarray(by_offset[::-1].copy()), most - here, bands, 0)
    fwd_hr, fwd_hi = dft_tables(TH, -1.0)
    fwd_h = jnp.asarray(np.concatenate([fwd_hr, fwd_hi], axis=0))
    row_w = jnp.concatenate([weights, weights], axis=1)
    tables = (row_w[:, :, None] * fwd_h[None].astype(jnp.float32)).astype(jnp.bfloat16)
    tables = jnp.transpose(tables, (1, 0, 2)).reshape(2 * TH, bands * TH)
    fwd_w = jnp.asarray(np.concatenate(dft_tables(TW, -1.0), axis=1))
    return backward(forward(incoming, tables, fwd_w, wide_count))


def solution(mesh):
    in_specs = (
        P(("wide", "narrow"), None),
        P(None, ("wide", "narrow")),
        P(("wide", "narrow"), None),
        P(("wide", "narrow")),
        P(("wide", "narrow")),
    )
    out_specs = P(None, "narrow", "wide")
    return jax.shard_map(local, mesh=mesh, in_specs=in_specs, out_specs=out_specs, check_vma=False)
```

```python
import functools
import math

import jax
import jax.numpy as jnp
import numpy as np
from jax import lax
from jax.experimental import pallas as pl
from jax.experimental.pallas import tpu as pltpu
from jax.sharding import PartitionSpec as P

TH = 512
TW = 256
FACET = 16
DEPTH = 1280
REACH = 2
SPREAD = 16.0
PIXELS = FACET * FACET
WORDS = 2 * PIXELS + 128


def dft_tables(length, spin_sign):
    position = np.arange(length)
    angles = (position[:, None] * position[None, :] % length) * (2.0 * math.pi / length)
    as_bf16 = lambda v: np.asarray(v, np.float32).astype(jnp.bfloat16)
    return as_bf16(np.cos(angles)), as_bf16(spin_sign * np.sin(angles))


def signed_frequency(length):
    return (np.arange(length) + length // 2) % length - length // 2


def reach_weight(length, offset):
    travel = signed_frequency(length) * (DEPTH / (length * length))
    return np.exp(-((travel - offset) ** 2) / SPREAD).astype(np.float32)


def depth_phase(length):
    frequency = signed_frequency(length)
    return (DEPTH * frequency * frequency % (2 * length * length)) * (-math.pi / (length * length))


def render_into(amp_ref, par_ref, out_ref):
    par = par_ref[...]
    tilt_r, tilt_c, lead = par[:, 0:1], par[:, 1:2], par[:, 2:3]
    owner, row_at, col_at = par[:, 3:4], par[:, 4:5], par[:, 5:6]
    lane = lax.broadcasted_iota(jnp.int32, amp_ref.shape, 1)
    across = lane % FACET
    col_hi = jnp.floor(col_at * (1.0 / FACET))
    col_lo = col_at - FACET * col_hi
    row_hi = jnp.floor(row_at * (1.0 / FACET))
    row_lo = row_at - FACET * row_hi
    turn = col_lo.astype(jnp.int32)
    amp = amp_ref[...]
    for step in (1, 2, 4, 8):
        near = pltpu.roll(amp, step, 1)
        far = pltpu.roll(amp, PIXELS + step - FACET, 1)
        turned = jnp.where(across >= step, near, far)
        amp = jnp.where((turn & step) != 0, turned, amp)
    pixel = ((across - turn) & (FACET - 1)).astype(jnp.float32)
    phase = tilt_r * (lane // FACET).astype(jnp.float32) + tilt_c * pixel + lead
    real, imag = (amp * jnp.cos(phase)).astype(jnp.bfloat16), (amp * jnp.sin(phase)).astype(jnp.bfloat16)
    half = PIXELS // 2
    out_ref[:, 0:half] = real[:, :half]
    out_ref[:, half : 2 * half] = imag[:, :half]
    out_ref[:, 2 * half : 3 * half] = real[:, half:]
    out_ref[:, 3 * half : 4 * half] = imag[:, half:]
    spot = lax.broadcasted_iota(jnp.int32, (amp.shape[0], 128), 1)
    marks = jnp.where(spot == 0, owner, 0.0)
    for at, value in ((1, row_hi), (2, row_lo), (3, col_hi), (4, col_lo)):
        marks = jnp.where(spot == at, value, marks)
    out_ref[:, 4 * half :] = marks.astype(jnp.bfloat16)


MESH = pl.DeviceIdType.MESH


def greet(targets):
    barrier = pltpu.get_barrier_semaphore()
    for valid, target in targets:
        if valid is True:
            pl.semaphore_signal(barrier, inc=1, device_id=target, device_id_type=MESH)
        else:

            @pl.when(valid)
            def _():
                pl.semaphore_signal(barrier, inc=1, device_id=target, device_id_type=MESH)

    count = 0
    for valid, _ in targets:
        count = count + (1 if valid is True else valid.astype(jnp.int32))
    pl.semaphore_wait(barrier, count)


def front(
    wide, narrow, bands, per, meanwhile, amp_ref, par_ref, out_ref, gathered, outgoing, incoming, send_n, recv_n, send_w, recv_w
):
    column, band = lax.axis_index("wide"), lax.axis_index("narrow")
    block = outgoing.shape[1]

    def first_of(where):
        return jnp.clip(where - REACH, 0, narrow - bands)

    first = first_of(band)
    deltas = [d for d in range(-REACH, REACH + 1) if d != 0]
    targets = [((band + d >= 0) & (band + d < narrow), (column, band + d)) for d in deltas]
    peers = [(True, (lax.rem(column + step, wide), band)) for step in range(1, wide)]
    greet(targets + peers)
    render_into(amp_ref, par_ref, gathered.at[band - first])

    def narrow_copy(k):
        there = jnp.clip(band + deltas[k], 0, narrow - 1)
        return pltpu.make_async_remote_copy(
            src_ref=gathered.at[band - first],
            dst_ref=gathered.at[jnp.clip(band - first_of(there), 0, bands - 1)],
            send_sem=send_n.at[k],
            recv_sem=recv_n.at[k],
            device_id=(column, there),
            device_id_type=MESH,
        )

    for k in range(len(deltas)):

        @pl.when(targets[k][0])
        def _(k=k):
            narrow_copy(k).start()

    for i in range(bands):
        away = first + i - band

        @pl.when((away > REACH) | (away < -REACH))
        def _(i=i):
            gathered[i] = jnp.zeros(gathered.shape[1:], gathered.dtype)

    meanwhile()
    for k, d in enumerate(deltas):

        @pl.when((band - d >= 0) & (band - d < narrow))
        def _(k=k):
            narrow_copy(k).wait_recv()

    facets = amp_ref.shape[0]
    lane = lax.broadcasted_iota(jnp.int32, (facets, 128), 1)
    below = lax.broadcasted_iota(jnp.int32, (facets, facets), 0) > lax.broadcasted_iota(
        jnp.int32, (facets, facets), 1
    )
    earlier = jnp.where(below, 1.0, 0.0).astype(jnp.bfloat16)
    select = jnp.where(lax.broadcasted_iota(jnp.int32, (8, 128), 1) == 0, 1.0, 0.0).astype(jnp.bfloat16)
    spot = lax.broadcasted_iota(jnp.int32, (wide * per, facets), 0).astype(jnp.float32)
    sorted_by_owner = []
    for i in range(bands):
        packed = gathered[i]
        owner = packed[:, 2 * PIXELS :].astype(jnp.float32)[:, 0:1]
        chosen = jnp.where(lane.astype(jnp.float32) == owner, 1.0, 0.0)
        rank = jnp.sum(dot(earlier, chosen.astype(jnp.bfloat16)) * chosen, axis=1, keepdims=True)
        slot = jnp.where(lane == 0, owner * float(per) + rank, 0.0).astype(jnp.bfloat16)
        slot = lax.dot_general(
            select, slot, (((1,), (1,)), ((), ())), preferred_element_type=jnp.float32
        )[0:1]
        pick = jnp.where(spot == slot, 1.0, 0.0).astype(jnp.bfloat16)
        sorted_by_owner.append(dot(pick, packed))
    spare = block - bands * per
    for w in range(wide):
        pieces = [one[w * per : (w + 1) * per] for one in sorted_by_owner]
        if spare:
            pieces.append(jnp.zeros((spare, WORDS), jnp.float32))
        outgoing[w] = jnp.concatenate(pieces, axis=0).astype(jnp.bfloat16)

    def wide_copy(step):
        there = lax.rem(column + step, wide)
        return pltpu.make_async_remote_copy(
            src_ref=outgoing.at[there],
            dst_ref=incoming.at[column],
            send_sem=send_w.at[step],
            recv_sem=recv_w.at[step],
            device_id=(there, band),
            device_id_type=MESH,
        )

    for step in range(1, wide):
        wide_copy(step).start()
    incoming[column] = outgoing[column]
    for step in range(1, wide):
        wide_copy(step).wait_recv()
    blocks = [incoming[w].astype(jnp.float32) for w in range(wide)]
    for i in range(bands):
        rows = jnp.concatenate([one[i * per : (i + 1) * per] for one in blocks], axis=0)
        out_ref[i * wide * per : (i + 1) * wide * per, :] = rows.astype(jnp.bfloat16)
    for step in range(1, wide):
        wide_copy(step).wait_send()
    for k in range(len(deltas)):

        @pl.when(targets[k][0])
        def _(k=k):
            narrow_copy(k).wait_send()


def dot(a, b):
    return jnp.dot(a, b, preferred_element_type=jnp.float32)


def fill_tiles(tile_ref):
    half = PIXELS // 2
    lane = lax.broadcasted_iota(jnp.int32, tile_ref.shape[1:], 0)
    spot = lax.broadcasted_iota(jnp.int32, tile_ref.shape[1:], 1)
    same = (lane // half == spot // TW) & (lane % FACET == spot % FACET)
    group = jnp.where(same, lane % half // FACET, -1)
    for at in range(FACET // 2):
        tile_ref[at] = jnp.where(group == at, 1.0, 0.0).astype(jnp.bfloat16)


def forward(bands, slots, here, pay_ref, tile_ref, tab_ref, weight_ref, wide_ref, out_ref, mask, spread, plane, total):
    half = PIXELS
    marks = pay_ref[:, 2 * PIXELS :].astype(jnp.float32)
    col_at = FACET * marks[:, 3:4] + marks[:, 4:5]
    spot = (lax.broadcasted_iota(jnp.int32, mask.shape, 1) % TW).astype(jnp.float32) - col_at
    mask[...] = jnp.where((spot >= 0.0) & (spot < FACET), 1.0, 0.0).astype(jnp.bfloat16)
    for side in range(2):
        fields = pay_ref[:, side * half : (side + 1) * half]

        def widen(at, _):
            pixels = dot(fields, tile_ref[at]).astype(jnp.bfloat16) * mask[...]
            row = pl.multiple_of((side * (FACET // 2) + at) * slots, slots)
            for b in range(bands):
                spread[b, pl.ds(row, slots), :] = pixels[b * slots : (b + 1) * slots]
            return 0

        lax.fori_loop(0, FACET // 2, widen, 0)
    lane = lax.broadcasted_iota(jnp.int32, (8, 128), 1)
    select = jnp.where(lane == 1, float(FACET), jnp.where(lane == 2, 1.0, 0.0)).astype(jnp.bfloat16)
    group = 8
    depth = group * slots
    spot = lax.broadcasted_iota(jnp.int32, (TH, depth), 0).astype(jnp.float32)
    for b in range(bands):
        corner = pay_ref[b * slots : (b + 1) * slots, 2 * PIXELS :]
        row_at = lax.dot_general(
            select, corner, (((1,), (1,)), ((), ())), preferred_element_type=jnp.float32
        )[0:1]
        row_at = jnp.concatenate([row_at + float(u) for u in range(group)], axis=1)
        for at in range(FACET // group):
            hot = jnp.where(spot == row_at + float(at * group), 1.0, 0.0).astype(jnp.bfloat16)
            part = dot(hot, spread[b, at * depth : (at + 1) * depth, :])
            plane[...] = part if at == 0 else plane[...] + part
        place = lax.broadcasted_iota(jnp.int32, weight_ref.shape, 1) - 2 * REACH
        weight = jnp.sum(jnp.where(place == here - b, weight_ref[...], 0.0), axis=1, keepdims=True)
        source = plane[...].astype(jnp.bfloat16)
        for part in range(2):
            half = slice(part * TH, (part + 1) * TH)
            rows = weight * dot(tab_ref[half, :], source)
            total[half, :] = rows if b == 0 else total[half, :] + rows
    scale = 1.0 / math.sqrt(TH * TW)
    real = (total[:TH, :TW] - total[TH:, TW:]).astype(jnp.bfloat16)
    imag = (total[:TH, TW:] + total[TH:, :TW]).astype(jnp.bfloat16)
    by_real, by_imag = dot(real, wide_ref[...]), dot(imag, wide_ref[...])
    spec_r = (by_real[:, :TW] - by_imag[:, TW:]) * scale
    spec_i = (by_real[:, TW:] + by_imag[:, :TW]) * scale
    wide, rows = out_ref.shape[0], out_ref.shape[1] // 2
    for w in range(wide):
        here = slice(w * rows, (w + 1) * rows)
        out_ref[w] = jnp.concatenate([spec_r[here], spec_i[here]], axis=0).astype(jnp.bfloat16)


def backward(
    wide, arrive, spec_ref, weight_ref, phase, wide_ref, high_ref, out_ref,
    parts, focus, back, image, send_a, recv_a, send_b, recv_b,
):
    column, band = lax.axis_index("wide"), lax.axis_index("narrow")
    rows = TH // wide

    def copy(step, source, landing, send, recv):
        there = lax.rem(column + step, wide)
        return pltpu.make_async_remote_copy(
            src_ref=source.at[there],
            dst_ref=landing.at[column],
            send_sem=send.at[step],
            recv_sem=recv.at[step],
            device_id=(there, band),
            device_id_type=MESH,
        )

    def out_copy(step):
        return copy(step, spec_ref, parts, send_a, recv_a)

    def home_copy(step):
        return copy(step, focus, back, send_b, recv_b)

    for step in range(1, wide):
        out_copy(step).start()
    parts[column] = spec_ref[column]
    arrive()
    phase_r, phase_i = phase[0], phase[1]
    for step in range(1, wide):
        out_copy(step).wait_recv()
    for step in list(range(1, wide)) + [0]:
        there = lax.rem(column + step, wide)
        total = None
        for offset in range(-REACH, REACH + 1):
            source = there - offset
            inside = jnp.where((source >= 0) & (source < wide), 1.0, 0.0)
            weight = weight_ref[offset + REACH : offset + REACH + 1, :] * inside
            term = weight * parts[jnp.clip(source, 0, wide - 1)].astype(jnp.float32)
            total = term if total is None else total + term
        real, imag = total[:rows], total[rows:]
        turned = jnp.concatenate(
            [phase_r * real - phase_i * imag, phase_r * imag + phase_i * real], axis=0
        ).astype(jnp.bfloat16)
        if step:
            focus[there] = turned
            home_copy(step).start()
        else:
            back[column] = turned
    for step in range(wide):
        source = lax.rem(column - step + wide, wide)
        if step:
            home_copy(step).wait_recv()
        both = dot(back[source], wide_ref[...])
        top, low = both[:rows], both[rows:]
        image[source, :, :TW] = top[:, :TW] - low[:, TW:]
        image[source, :, TW:] = top[:, TW:] + low[:, :TW]
    scale = 1.0 / math.sqrt(TH * TW)
    pair = image[...].reshape(TH, 2 * TW).astype(jnp.bfloat16)
    top, low = dot(high_ref[:TH], pair), dot(high_ref[TH:], pair)
    out_ref[0] = (top[:, :TW] - low[:, TW:]) * scale
    out_ref[1] = (top[:, TW:] + low[:, :TW]) * scale
    for step in range(1, wide):
        out_copy(step).wait_send()
        home_copy(step).wait_send()


def whole_kernel(
    wide, narrow, bands, per,
    amp_ref, par_ref, row_weight, col_weight, fwd_w, inv_w, phase_all, fwd_h_all, inv_h_all, out_ref,
    gathered, outgoing, incoming, send_n, recv_n, send_w, recv_w,
    pay, tiles, mask, spread, plane, total, spec,
    parts, focus, back, image, send_a, recv_a, send_b, recv_b,
    phase, fwd_h, inv_h, load,
):
    column, band = lax.axis_index("wide"), lax.axis_index("narrow")
    rows = TH // wide
    own = pl.ds(pl.multiple_of(column * rows, rows), rows)
    fetch_tab = pltpu.make_async_copy(fwd_h_all, fwd_h, load.at[0])
    fetch_phase = pltpu.make_async_copy(phase_all.at[:, own, :], phase, load.at[1])
    fetch_inv = pltpu.make_async_copy(inv_h_all, inv_h, load.at[2])
    for one in (fetch_tab, fetch_phase, fetch_inv):
        one.start()
    front(
        wide, narrow, bands, per, lambda: fill_tiles(tiles),
        amp_ref, par_ref, pay, gathered, outgoing, incoming, send_n, recv_n, send_w, recv_w,
    )
    fetch_tab.wait()
    here = band - jnp.clip(band - REACH, 0, narrow - bands)
    forward(
        bands, wide * per, here, pay, tiles, fwd_h, row_weight, fwd_w, spec, mask, spread, plane, total
    )

    def arrive():
        fetch_phase.wait()
        fetch_inv.wait()

    backward(
        wide, arrive, spec, col_weight, phase, inv_w, inv_h, out_ref,
        parts, focus, back, image, send_a, recv_a, send_b, recv_b,
    )


def local(amplitude, tilt, owner, row_offset, col_offset):
    wide, narrow = lax.axis_size("wide"), lax.axis_size("narrow")
    facets = amplitude.shape[0]
    per = max(2, (3 * facets + wide - 1) // wide)
    bands = min(narrow, 2 * REACH + 1)
    slots = wide * per
    block = (bands * per + 15) // 16 * 16
    rows = TH // wide
    par = jnp.concatenate(
        [tilt, jnp.stack([owner[:, 0], row_offset, col_offset]).astype(jnp.float32)], axis=0
    )
    par = jnp.pad(par.T, ((0, 0), (0, 2)))
    row_weight = np.zeros((TH, 128), np.float32)
    col_weight = np.zeros((8, TW), np.float32)
    for offset in range(-REACH, REACH + 1):
        row_weight[:, 2 * REACH + offset] = reach_weight(TH, float(offset))
        col_weight[offset + REACH] = reach_weight(TW, float(offset))
    angle = depth_phase(TH)[:, None] + depth_phase(TW)[None, :]
    phase = np.stack([np.cos(angle), np.sin(angle)]).astype(np.float32)
    constants = [
        row_weight,
        col_weight,
        np.concatenate(dft_tables(TW, -1.0), axis=1),
        np.concatenate(dft_tables(TW, 1.0), axis=1),
        phase,
        np.concatenate(dft_tables(TH, -1.0), axis=0),
        np.concatenate(dft_tables(TH, 1.0), axis=0),
    ]
    dma = lambda count: pltpu.SemaphoreType.DMA((count,))
    narrow16 = lambda *shape: pltpu.VMEM(shape, jnp.bfloat16)
    wide32 = lambda *shape: pltpu.VMEM(shape, jnp.float32)
    return pl.pallas_call(
        functools.partial(whole_kernel, wide, narrow, bands, per),
        out_shape=jax.ShapeDtypeStruct((2, TH, TW), jnp.float32),
        in_specs=[pl.BlockSpec(memory_space=pltpu.VMEM)] * 6 + [pl.BlockSpec(memory_space=pl.ANY)] * 3,
        out_specs=pl.BlockSpec(memory_space=pltpu.VMEM),
        scratch_shapes=[
            narrow16(bands, facets, WORDS),
            narrow16(wide, block, WORDS),
            narrow16(wide, block, WORDS),
            dma(2 * REACH),
            dma(2 * REACH),
            dma(wide),
            dma(wide),
            narrow16(bands * slots, WORDS),
            narrow16(FACET // 2, PIXELS, 2 * TW),
            narrow16(bands * slots, 2 * TW),
            narrow16(bands, FACET * slots, 2 * TW),
            wide32(TH, 2 * TW),
            wide32(2 * TH, 2 * TW),
            narrow16(wide, 2 * rows, TW),
            narrow16(wide, 2 * rows, TW),
            narrow16(wide, 2 * rows, TW),
            narrow16(wide, 2 * rows, TW),
            wide32(wide, rows, 2 * TW),
            dma(wide),
            dma(wide),
            dma(wide),
            dma(wide),
            wide32(2, rows, TW),
            narrow16(2 * TH, TH),
            narrow16(2 * TH, TH),
            dma(3),
        ],
        compiler_params=pltpu.CompilerParams(
            collective_id=0, has_side_effects=True, vmem_limit_bytes=56 * 2**20
        ),
    )(amplitude, par, *[jnp.asarray(one) for one in constants])


def solution(mesh):
    in_specs = (
        P(("wide", "narrow"), None),
        P(None, ("wide", "narrow")),
        P(("wide", "narrow"), None),
        P(("wide", "narrow")),
        P(("wide", "narrow")),
    )
    out_specs = P(None, "narrow", "wide")
    return jax.shard_map(local, mesh=mesh, in_specs=in_specs, out_specs=out_specs, check_vma=False)
```

```python
import functools
import math

import jax
import jax.numpy as jnp
import numpy as np
from jax import lax
from jax.experimental import pallas as pl
from jax.experimental.pallas import tpu as pltpu
from jax.sharding import PartitionSpec as P

TH = 512
TW = 256
FACET = 16
DEPTH = 1280
REACH = 2
SPREAD = 16.0
PIXELS = FACET * FACET
PARTS = (PIXELS + 128, PIXELS)


def dft_tables(length, spin_sign):
    position = np.arange(length)
    angles = (position[:, None] * position[None, :] % length) * (2.0 * math.pi / length)
    as_bf16 = lambda v: np.asarray(v, np.float32).astype(jnp.bfloat16)
    return as_bf16(np.cos(angles)), as_bf16(spin_sign * np.sin(angles))


def signed_frequency(length):
    return (np.arange(length) + length // 2) % length - length // 2


def reach_weight(length, offset):
    travel = signed_frequency(length) * (DEPTH / (length * length))
    return np.exp(-((travel - offset) ** 2) / SPREAD).astype(np.float32)


def depth_phase(length):
    frequency = signed_frequency(length)
    return (DEPTH * frequency * frequency % (2 * length * length)) * (-math.pi / (length * length))


def render_into(amp_ref, par_ref, low_ref, high_ref):
    par = par_ref[...]
    tilt_r, tilt_c, lead = par[:, 0:1], par[:, 1:2], par[:, 2:3]
    owner, row_at, col_at = par[:, 3:4], par[:, 4:5], par[:, 5:6]
    lane = lax.broadcasted_iota(jnp.int32, amp_ref.shape, 1)
    across = lane % FACET
    col_hi = jnp.floor(col_at * (1.0 / FACET))
    col_lo = col_at - FACET * col_hi
    row_hi = jnp.floor(row_at * (1.0 / FACET))
    row_lo = row_at - FACET * row_hi
    turn = col_lo.astype(jnp.int32)
    amp = amp_ref[...]
    for step in (1, 2, 4, 8):
        near = pltpu.roll(amp, step, 1)
        far = pltpu.roll(amp, PIXELS + step - FACET, 1)
        turned = jnp.where(across >= step, near, far)
        amp = jnp.where((turn & step) != 0, turned, amp)
    pixel = ((across - turn) & (FACET - 1)).astype(jnp.float32)
    phase = tilt_r * (lane // FACET).astype(jnp.float32) + tilt_c * pixel + lead
    real, imag = (amp * jnp.cos(phase)).astype(jnp.bfloat16), (amp * jnp.sin(phase)).astype(jnp.bfloat16)
    half = PIXELS // 2
    low_ref[:, 0:half] = real[:, half:]
    low_ref[:, half : 2 * half] = imag[:, half:]
    high_ref[:, 0:half] = real[:, :half]
    high_ref[:, half : 2 * half] = imag[:, :half]
    spot = lax.broadcasted_iota(jnp.int32, (amp.shape[0], 128), 1)
    marks = jnp.where(spot == 0, owner, 0.0)
    for at, value in ((1, row_hi), (2, row_lo), (3, col_hi), (4, col_lo)):
        marks = jnp.where(spot == at, value, marks)
    low_ref[:, 2 * half :] = marks.astype(jnp.bfloat16)


MESH = pl.DeviceIdType.MESH


def greet(targets):
    barrier = pltpu.get_barrier_semaphore()
    for valid, target in targets:
        if valid is True:
            pl.semaphore_signal(barrier, inc=1, device_id=target, device_id_type=MESH)
        else:

            @pl.when(valid)
            def _():
                pl.semaphore_signal(barrier, inc=1, device_id=target, device_id_type=MESH)

    count = 0
    for valid, _ in targets:
        count = count + (1 if valid is True else valid.astype(jnp.int32))
    pl.semaphore_wait(barrier, count)


def front(
    wide, narrow, bands, per, meanwhile, amp_ref, par_ref, out_ref, gathered, outgoing, incoming, send_n, recv_n, send_w, recv_w
):
    column, band = lax.axis_index("wide"), lax.axis_index("narrow")
    block = outgoing[0].shape[1]

    def first_of(where):
        return jnp.clip(where - REACH, 0, narrow - bands)

    first = first_of(band)
    deltas = [d for d in range(-REACH, REACH + 1) if d != 0]
    targets = [((band + d >= 0) & (band + d < narrow), (column, band + d)) for d in deltas]
    peers = [(True, (lax.rem(column + step, wide), band)) for step in range(1, wide)]
    greet(targets + peers)
    render_into(amp_ref, par_ref, gathered[0].at[band - first], gathered[1].at[band - first])

    def narrow_copy(part, k):
        there = jnp.clip(band + deltas[k], 0, narrow - 1)
        return pltpu.make_async_remote_copy(
            src_ref=gathered[part].at[band - first],
            dst_ref=gathered[part].at[jnp.clip(band - first_of(there), 0, bands - 1)],
            send_sem=send_n.at[part, k],
            recv_sem=recv_n.at[part, k],
            device_id=(column, there),
            device_id_type=MESH,
        )

    for part in range(2):
        for k in range(len(deltas)):

            @pl.when(targets[k][0])
            def _(part=part, k=k):
                narrow_copy(part, k).start()

    for i in range(bands):
        away = first + i - band

        @pl.when((away > REACH) | (away < -REACH))
        def _(i=i):
            for one in gathered:
                one[i] = jnp.zeros(one.shape[1:], one.dtype)

    meanwhile()

    def narrow_arrive(part):
        for k, d in enumerate(deltas):

            @pl.when((band - d >= 0) & (band - d < narrow))
            def _(k=k):
                narrow_copy(part, k).wait_recv()

    narrow_arrive(0)
    facets = amp_ref.shape[0]
    lane = lax.broadcasted_iota(jnp.int32, (facets, 128), 1)
    below = lax.broadcasted_iota(jnp.int32, (facets, facets), 0) > lax.broadcasted_iota(
        jnp.int32, (facets, facets), 1
    )
    earlier = jnp.where(below, 1.0, 0.0).astype(jnp.bfloat16)
    select = jnp.where(lax.broadcasted_iota(jnp.int32, (8, 128), 1) == 0, 1.0, 0.0).astype(jnp.bfloat16)
    spot = lax.broadcasted_iota(jnp.int32, (wide * per, facets), 0).astype(jnp.float32)
    picks = []
    for i in range(bands):
        owner = gathered[0][i][:, PIXELS:].astype(jnp.float32)[:, 0:1]
        chosen = jnp.where(lane.astype(jnp.float32) == owner, 1.0, 0.0)
        rank = jnp.sum(dot(earlier, chosen.astype(jnp.bfloat16)) * chosen, axis=1, keepdims=True)
        slot = jnp.where(lane == 0, owner * float(per) + rank, 0.0).astype(jnp.bfloat16)
        slot = lax.dot_general(
            select, slot, (((1,), (1,)), ((), ())), preferred_element_type=jnp.float32
        )[0:1]
        picks.append(jnp.where(spot == slot, 1.0, 0.0).astype(jnp.bfloat16))
    spare = block - bands * per

    def wide_copy(part, step):
        there = lax.rem(column + step, wide)
        return pltpu.make_async_remote_copy(
            src_ref=outgoing[part].at[there],
            dst_ref=incoming[part].at[column],
            send_sem=send_w.at[part, step],
            recv_sem=recv_w.at[part, step],
            device_id=(there, band),
            device_id_type=MESH,
        )

    for part in range(2):
        if part:
            narrow_arrive(part)
        by_owner = [dot(picks[i], gathered[part][i]) for i in range(bands)]
        for w in range(wide):
            pieces = [one[w * per : (w + 1) * per] for one in by_owner]
            if spare:
                pieces.append(jnp.zeros((spare, PARTS[part]), jnp.float32))
            outgoing[part][w] = jnp.concatenate(pieces, axis=0).astype(jnp.bfloat16)
        for step in range(1, wide):
            wide_copy(part, step).start()
        incoming[part][column] = outgoing[part][column]

    def arrive(part):
        for step in range(1, wide):
            wide_copy(part, step).wait_recv()
        blocks = [incoming[part][w].astype(jnp.float32) for w in range(wide)]
        for i in range(bands):
            rows = jnp.concatenate([one[i * per : (i + 1) * per] for one in blocks], axis=0)
            out_ref[part][i * wide * per : (i + 1) * wide * per, :] = rows.astype(jnp.bfloat16)

    def finish():
        for part in range(2):
            for step in range(1, wide):
                wide_copy(part, step).wait_send()
            for k in range(len(deltas)):

                @pl.when(targets[k][0])
                def _(part=part, k=k):
                    narrow_copy(part, k).wait_send()

    return arrive, finish


def dot(a, b):
    return jnp.dot(a, b, preferred_element_type=jnp.float32)


def fill_tiles(tile_ref):
    half = PIXELS // 2
    lane = lax.broadcasted_iota(jnp.int32, tile_ref.shape[1:], 0)
    spot = lax.broadcasted_iota(jnp.int32, tile_ref.shape[1:], 1)
    same = (lane // half == spot // TW) & (lane % FACET == spot % FACET)
    group = jnp.where(same, lane % half // FACET, -1)
    for at in range(FACET // 2):
        tile_ref[at] = jnp.where(group == at, 1.0, 0.0).astype(jnp.bfloat16)


def forward(bands, slots, here, arrive, pay_ref, tile_ref, tab_ref, weight_ref, wide_ref, out_ref, mask, spread, plane, total):
    arrive(0)
    marks = pay_ref[0][:, PIXELS:].astype(jnp.float32)
    col_at = FACET * marks[:, 3:4] + marks[:, 4:5]
    spot = (lax.broadcasted_iota(jnp.int32, mask.shape, 1) % TW).astype(jnp.float32) - col_at
    mask[...] = jnp.where((spot >= 0.0) & (spot < FACET), 1.0, 0.0).astype(jnp.bfloat16)
    for part, side in ((0, 1), (1, 0)):
        if part:
            arrive(part)
        fields = pay_ref[part][:, :PIXELS]

        def widen(at, _, fields=fields, side=side):
            pixels = dot(fields, tile_ref[at]).astype(jnp.bfloat16) * mask[...]
            row = pl.multiple_of((side * (FACET // 2) + at) * slots, slots)
            for b in range(bands):
                spread[b, pl.ds(row, slots), :] = pixels[b * slots : (b + 1) * slots]
            return 0

        lax.fori_loop(0, FACET // 2, widen, 0)
    lane = lax.broadcasted_iota(jnp.int32, (8, 128), 1)
    select = jnp.where(lane == 1, float(FACET), jnp.where(lane == 2, 1.0, 0.0)).astype(jnp.bfloat16)
    group = 8
    depth = group * slots
    spot = lax.broadcasted_iota(jnp.int32, (TH, depth), 0).astype(jnp.float32)
    for b in range(bands):
        corner = pay_ref[0][b * slots : (b + 1) * slots, PIXELS:]
        row_at = lax.dot_general(
            select, corner, (((1,), (1,)), ((), ())), preferred_element_type=jnp.float32
        )[0:1]
        row_at = jnp.concatenate([row_at + float(u) for u in range(group)], axis=1)
        for at in range(FACET // group):
            hot = jnp.where(spot == row_at + float(at * group), 1.0, 0.0).astype(jnp.bfloat16)
            part = dot(hot, spread[b, at * depth : (at + 1) * depth, :])
            plane[...] = part if at == 0 else plane[...] + part
        place = lax.broadcasted_iota(jnp.int32, weight_ref.shape, 1) - 2 * REACH
        weight = jnp.sum(jnp.where(place == here - b, weight_ref[...], 0.0), axis=1, keepdims=True)
        source = plane[...].astype(jnp.bfloat16)
        for part in range(2):
            half = slice(part * TH, (part + 1) * TH)
            rows = weight * dot(tab_ref[half, :], source)
            total[half, :] = rows if b == 0 else total[half, :] + rows
    scale = 1.0 / math.sqrt(TH * TW)
    real = (total[:TH, :TW] - total[TH:, TW:]).astype(jnp.bfloat16)
    imag = (total[:TH, TW:] + total[TH:, :TW]).astype(jnp.bfloat16)
    by_real, by_imag = dot(real, wide_ref[...]), dot(imag, wide_ref[...])
    spec_r = (by_real[:, :TW] - by_imag[:, TW:]) * scale
    spec_i = (by_real[:, TW:] + by_imag[:, :TW]) * scale
    wide, rows = out_ref.shape[0], out_ref.shape[1] // 2
    for w in range(wide):
        here = slice(w * rows, (w + 1) * rows)
        out_ref[w] = jnp.concatenate([spec_r[here], spec_i[here]], axis=0).astype(jnp.bfloat16)


def backward(
    wide, arrive, spec_ref, weight_ref, phase, wide_ref, high_ref, out_ref,
    parts, focus, back, image, send_a, recv_a, send_b, recv_b,
):
    column, band = lax.axis_index("wide"), lax.axis_index("narrow")
    rows = TH // wide

    def copy(step, source, landing, send, recv):
        there = lax.rem(column + step, wide)
        return pltpu.make_async_remote_copy(
            src_ref=source.at[there],
            dst_ref=landing.at[column],
            send_sem=send.at[step],
            recv_sem=recv.at[step],
            device_id=(there, band),
            device_id_type=MESH,
        )

    def out_copy(step):
        return copy(step, spec_ref, parts, send_a, recv_a)

    def home_copy(step):
        return copy(step, focus, back, send_b, recv_b)

    for step in range(1, wide):
        out_copy(step).start()
    parts[column] = spec_ref[column]
    arrive()
    phase_r, phase_i = phase[0], phase[1]
    for step in range(1, wide):
        out_copy(step).wait_recv()
    for step in list(range(1, wide)) + [0]:
        there = lax.rem(column + step, wide)
        total = None
        for offset in range(-REACH, REACH + 1):
            source = there - offset
            inside = jnp.where((source >= 0) & (source < wide), 1.0, 0.0)
            weight = weight_ref[offset + REACH : offset + REACH + 1, :] * inside
            term = weight * parts[jnp.clip(source, 0, wide - 1)].astype(jnp.float32)
            total = term if total is None else total + term
        real, imag = total[:rows], total[rows:]
        turned = jnp.concatenate(
            [phase_r * real - phase_i * imag, phase_r * imag + phase_i * real], axis=0
        ).astype(jnp.bfloat16)
        if step:
            focus[there] = turned
            home_copy(step).start()
        else:
            back[column] = turned
    for step in range(wide):
        source = lax.rem(column - step + wide, wide)
        if step:
            home_copy(step).wait_recv()
        both = dot(back[source], wide_ref[...])
        top, low = both[:rows], both[rows:]
        image[source, :, :TW] = top[:, :TW] - low[:, TW:]
        image[source, :, TW:] = top[:, TW:] + low[:, :TW]
    scale = 1.0 / math.sqrt(TH * TW)
    pair = image[...].reshape(TH, 2 * TW).astype(jnp.bfloat16)
    top, low = dot(high_ref[:TH], pair), dot(high_ref[TH:], pair)
    out_ref[0] = (top[:, :TW] - low[:, TW:]) * scale
    out_ref[1] = (top[:, TW:] + low[:, :TW]) * scale
    for step in range(1, wide):
        out_copy(step).wait_send()
        home_copy(step).wait_send()


def whole_kernel(
    wide, narrow, bands, per,
    amp_ref, par_ref, row_weight, col_weight, fwd_w, inv_w, phase_all, fwd_h_all, inv_h_all, out_ref,
    gathered_a, gathered_b, outgoing_a, outgoing_b, incoming_a, incoming_b, send_n, recv_n, send_w, recv_w,
    pay_a, pay_b, tiles, mask, spread, plane, total, spec,
    parts, focus, back, image, send_a, recv_a, send_b, recv_b,
    phase, fwd_h, inv_h, load,
):
    column, band = lax.axis_index("wide"), lax.axis_index("narrow")
    rows = TH // wide
    own = pl.ds(pl.multiple_of(column * rows, rows), rows)
    fetch_tab = pltpu.make_async_copy(fwd_h_all, fwd_h, load.at[0])
    fetch_phase = pltpu.make_async_copy(phase_all.at[:, own, :], phase, load.at[1])
    fetch_inv = pltpu.make_async_copy(inv_h_all, inv_h, load.at[2])
    for one in (fetch_tab, fetch_phase, fetch_inv):
        one.start()
    pay = (pay_a, pay_b)
    landed, finish = front(
        wide, narrow, bands, per, lambda: fill_tiles(tiles), amp_ref, par_ref, pay,
        (gathered_a, gathered_b), (outgoing_a, outgoing_b), (incoming_a, incoming_b),
        send_n, recv_n, send_w, recv_w,
    )
    fetch_tab.wait()
    here = band - jnp.clip(band - REACH, 0, narrow - bands)
    forward(
        bands, wide * per, here, landed, pay, tiles, fwd_h, row_weight, fwd_w, spec, mask, spread, plane, total
    )

    def arrive():
        fetch_phase.wait()
        fetch_inv.wait()

    backward(
        wide, arrive, spec, col_weight, phase, inv_w, inv_h, out_ref,
        parts, focus, back, image, send_a, recv_a, send_b, recv_b,
    )
    finish()


def local(amplitude, tilt, owner, row_offset, col_offset):
    wide, narrow = lax.axis_size("wide"), lax.axis_size("narrow")
    facets = amplitude.shape[0]
    per = max(2, (3 * facets + wide - 1) // wide)
    bands = min(narrow, 2 * REACH + 1)
    slots = wide * per
    block = (bands * per + 15) // 16 * 16
    rows = TH // wide
    par = jnp.concatenate(
        [tilt, jnp.stack([owner[:, 0], row_offset, col_offset]).astype(jnp.float32)], axis=0
    )
    par = jnp.pad(par.T, ((0, 0), (0, 2)))
    row_weight = np.zeros((TH, 128), np.float32)
    col_weight = np.zeros((8, TW), np.float32)
    for offset in range(-REACH, REACH + 1):
        row_weight[:, 2 * REACH + offset] = reach_weight(TH, float(offset))
        col_weight[offset + REACH] = reach_weight(TW, float(offset))
    angle = depth_phase(TH)[:, None] + depth_phase(TW)[None, :]
    phase = np.stack([np.cos(angle), np.sin(angle)]).astype(np.float32)
    constants = [
        row_weight,
        col_weight,
        np.concatenate(dft_tables(TW, -1.0), axis=1),
        np.concatenate(dft_tables(TW, 1.0), axis=1),
        phase,
        np.concatenate(dft_tables(TH, -1.0), axis=0),
        np.concatenate(dft_tables(TH, 1.0), axis=0),
    ]
    dma = lambda *shape: pltpu.SemaphoreType.DMA(shape)
    narrow16 = lambda *shape: pltpu.VMEM(shape, jnp.bfloat16)
    wide32 = lambda *shape: pltpu.VMEM(shape, jnp.float32)
    return pl.pallas_call(
        functools.partial(whole_kernel, wide, narrow, bands, per),
        out_shape=jax.ShapeDtypeStruct((2, TH, TW), jnp.float32),
        in_specs=[pl.BlockSpec(memory_space=pltpu.VMEM)] * 6 + [pl.BlockSpec(memory_space=pl.ANY)] * 3,
        out_specs=pl.BlockSpec(memory_space=pltpu.VMEM),
        scratch_shapes=[
            *[narrow16(bands, facets, words) for words in PARTS],
            *[narrow16(wide, block, words) for words in PARTS],
            *[narrow16(wide, block, words) for words in PARTS],
            dma(2, 2 * REACH),
            dma(2, 2 * REACH),
            dma(2, wide),
            dma(2, wide),
            *[narrow16(bands * slots, words) for words in PARTS],
            narrow16(FACET // 2, PIXELS, 2 * TW),
            narrow16(bands * slots, 2 * TW),
            narrow16(bands, FACET * slots, 2 * TW),
            wide32(TH, 2 * TW),
            wide32(2 * TH, 2 * TW),
            narrow16(wide, 2 * rows, TW),
            narrow16(wide, 2 * rows, TW),
            narrow16(wide, 2 * rows, TW),
            narrow16(wide, 2 * rows, TW),
            wide32(wide, rows, 2 * TW),
            dma(wide),
            dma(wide),
            dma(wide),
            dma(wide),
            wide32(2, rows, TW),
            narrow16(2 * TH, TH),
            narrow16(2 * TH, TH),
            dma(3),
        ],
        compiler_params=pltpu.CompilerParams(
            collective_id=0, has_side_effects=True, vmem_limit_bytes=56 * 2**20
        ),
    )(amplitude, par, *[jnp.asarray(one) for one in constants])


def solution(mesh):
    in_specs = (
        P(("wide", "narrow"), None),
        P(None, ("wide", "narrow")),
        P(("wide", "narrow"), None),
        P(("wide", "narrow")),
        P(("wide", "narrow")),
    )
    out_specs = P(None, "narrow", "wide")
    return jax.shard_map(local, mesh=mesh, in_specs=in_specs, out_specs=out_specs, check_vma=False)
```

```python
import functools
import math

import jax
import jax.numpy as jnp
import numpy as np
from jax import lax
from jax.experimental import pallas as pl
from jax.experimental.pallas import tpu as pltpu
from jax.sharding import PartitionSpec as P

TH = 512
TW = 256
FACET = 16
DEPTH = 1280
REACH = 2
SPREAD = 16.0
PIXELS = FACET * FACET
PARTS = (PIXELS + 128, PIXELS)


def dft_tables(length, spin_sign):
    position = np.arange(length)
    angles = (position[:, None] * position[None, :] % length) * (2.0 * math.pi / length)
    as_bf16 = lambda v: np.asarray(v, np.float32).astype(jnp.bfloat16)
    return as_bf16(np.cos(angles)), as_bf16(spin_sign * np.sin(angles))


def signed_frequency(length):
    return (np.arange(length) + length // 2) % length - length // 2


def reach_weight(length, offset):
    travel = signed_frequency(length) * (DEPTH / (length * length))
    return np.exp(-((travel - offset) ** 2) / SPREAD).astype(np.float32)


def depth_phase(length):
    frequency = signed_frequency(length)
    return (DEPTH * frequency * frequency % (2 * length * length)) * (-math.pi / (length * length))


def render_into(amp_ref, par_ref, low_ref, high_ref):
    par = par_ref[...]
    tilt_r, tilt_c, lead = par[:, 0:1], par[:, 1:2], par[:, 2:3]
    owner, row_at, col_at = par[:, 3:4], par[:, 4:5], par[:, 5:6]
    lane = lax.broadcasted_iota(jnp.int32, amp_ref.shape, 1)
    across = lane % FACET
    col_hi = jnp.floor(col_at * (1.0 / FACET))
    col_lo = col_at - FACET * col_hi
    row_hi = jnp.floor(row_at * (1.0 / FACET))
    row_lo = row_at - FACET * row_hi
    turn = col_lo.astype(jnp.int32)
    amp = amp_ref[...]
    for step in (1, 2, 4, 8):
        near = pltpu.roll(amp, step, 1)
        far = pltpu.roll(amp, PIXELS + step - FACET, 1)
        turned = jnp.where(across >= step, near, far)
        amp = jnp.where((turn & step) != 0, turned, amp)
    pixel = ((across - turn) & (FACET - 1)).astype(jnp.float32)
    phase = tilt_r * (lane // FACET).astype(jnp.float32) + tilt_c * pixel + lead
    real, imag = (amp * jnp.cos(phase)).astype(jnp.bfloat16), (amp * jnp.sin(phase)).astype(jnp.bfloat16)
    half = PIXELS // 2
    low_ref[:, 0:half] = real[:, half:]
    low_ref[:, half : 2 * half] = imag[:, half:]
    high_ref[:, 0:half] = real[:, :half]
    high_ref[:, half : 2 * half] = imag[:, :half]
    spot = lax.broadcasted_iota(jnp.int32, (amp.shape[0], 128), 1)
    marks = jnp.where(spot == 0, owner, 0.0)
    for at, value in ((1, row_hi), (2, row_lo), (3, col_hi), (4, col_lo)):
        marks = jnp.where(spot == at, value, marks)
    low_ref[:, 2 * half :] = marks.astype(jnp.bfloat16)


MESH = pl.DeviceIdType.MESH


def greet(targets):
    barrier = pltpu.get_barrier_semaphore()
    for valid, target in targets:
        if valid is True:
            pl.semaphore_signal(barrier, inc=1, device_id=target, device_id_type=MESH)
        else:

            @pl.when(valid)
            def _():
                pl.semaphore_signal(barrier, inc=1, device_id=target, device_id_type=MESH)

    count = 0
    for valid, _ in targets:
        count = count + (1 if valid is True else valid.astype(jnp.int32))
    pl.semaphore_wait(barrier, count)


def front(
    wide, narrow, bands, per, meanwhile, amp_ref, par_ref, out_ref, gathered, outgoing, incoming, send_n, recv_n, send_w, recv_w
):
    column, band = lax.axis_index("wide"), lax.axis_index("narrow")
    block = outgoing[0].shape[1]

    def first_of(where):
        return jnp.clip(where - REACH, 0, narrow - bands)

    first = first_of(band)
    deltas = [d for d in range(-REACH, REACH + 1) if d != 0]
    targets = [((band + d >= 0) & (band + d < narrow), (column, band + d)) for d in deltas]
    peers = [(True, (lax.rem(column + step, wide), band)) for step in range(1, wide)]
    greet(targets + peers)
    render_into(amp_ref, par_ref, gathered[0].at[band - first], gathered[1].at[band - first])

    def narrow_copy(part, k):
        there = jnp.clip(band + deltas[k], 0, narrow - 1)
        return pltpu.make_async_remote_copy(
            src_ref=gathered[part].at[band - first],
            dst_ref=gathered[part].at[jnp.clip(band - first_of(there), 0, bands - 1)],
            send_sem=send_n.at[part, k],
            recv_sem=recv_n.at[part, k],
            device_id=(column, there),
            device_id_type=MESH,
        )

    for part in range(2):
        for k in range(len(deltas)):

            @pl.when(targets[k][0])
            def _(part=part, k=k):
                narrow_copy(part, k).start()

    for i in range(bands):
        away = first + i - band

        @pl.when((away > REACH) | (away < -REACH))
        def _(i=i):
            for one in gathered:
                one[i] = jnp.zeros(one.shape[1:], one.dtype)

    meanwhile()

    def narrow_arrive(part):
        for k, d in enumerate(deltas):

            @pl.when((band - d >= 0) & (band - d < narrow))
            def _(k=k):
                narrow_copy(part, k).wait_recv()

    narrow_arrive(0)
    facets = amp_ref.shape[0]
    lane = lax.broadcasted_iota(jnp.int32, (facets, 128), 1)
    below = lax.broadcasted_iota(jnp.int32, (facets, facets), 0) > lax.broadcasted_iota(
        jnp.int32, (facets, facets), 1
    )
    earlier = jnp.where(below, 1.0, 0.0).astype(jnp.bfloat16)
    select = jnp.where(lax.broadcasted_iota(jnp.int32, (8, 128), 1) == 0, 1.0, 0.0).astype(jnp.bfloat16)
    spot = lax.broadcasted_iota(jnp.int32, (wide * per, facets), 0).astype(jnp.float32)
    picks = []
    for i in range(bands):
        owner = gathered[0][i][:, PIXELS:].astype(jnp.float32)[:, 0:1]
        chosen = jnp.where(lane.astype(jnp.float32) == owner, 1.0, 0.0)
        rank = jnp.sum(dot(earlier, chosen.astype(jnp.bfloat16)) * chosen, axis=1, keepdims=True)
        slot = jnp.where(lane == 0, owner * float(per) + rank, 0.0).astype(jnp.bfloat16)
        slot = lax.dot_general(
            select, slot, (((1,), (1,)), ((), ())), preferred_element_type=jnp.float32
        )[0:1]
        picks.append(jnp.where(spot == slot, 1.0, 0.0).astype(jnp.bfloat16))
    spare = block - bands * per

    def wide_copy(part, step):
        there = lax.rem(column + step, wide)
        return pltpu.make_async_remote_copy(
            src_ref=outgoing[part].at[there],
            dst_ref=incoming[part].at[column],
            send_sem=send_w.at[part, step],
            recv_sem=recv_w.at[part, step],
            device_id=(there, band),
            device_id_type=MESH,
        )

    for part in range(2):
        if part:
            narrow_arrive(part)
        by_owner = [dot(picks[i], gathered[part][i]) for i in range(bands)]
        for w in range(wide):
            pieces = [one[w * per : (w + 1) * per] for one in by_owner]
            if spare:
                pieces.append(jnp.zeros((spare, PARTS[part]), jnp.float32))
            outgoing[part][w] = jnp.concatenate(pieces, axis=0).astype(jnp.bfloat16)
        for step in range(1, wide):
            wide_copy(part, step).start()
        incoming[part][column] = outgoing[part][column]

    def arrive(part):
        for step in range(1, wide):
            wide_copy(part, step).wait_recv()
        blocks = [incoming[part][w].astype(jnp.float32) for w in range(wide)]
        for i in range(bands):
            rows = jnp.concatenate([one[i * per : (i + 1) * per] for one in blocks], axis=0)
            out_ref[part][i * wide * per : (i + 1) * wide * per, :] = rows.astype(jnp.bfloat16)

    def finish():
        for part in range(2):
            for step in range(1, wide):
                wide_copy(part, step).wait_send()
            for k in range(len(deltas)):

                @pl.when(targets[k][0])
                def _(part=part, k=k):
                    narrow_copy(part, k).wait_send()

    return arrive, finish


def dot(a, b):
    return jnp.dot(a, b, preferred_element_type=jnp.float32)


def fill_tiles(tile_ref):
    half = PIXELS // 2
    lane = lax.broadcasted_iota(jnp.int32, tile_ref.shape[1:], 0)
    spot = lax.broadcasted_iota(jnp.int32, tile_ref.shape[1:], 1)
    same = (lane // half == spot // TW) & (lane % FACET == spot % FACET)
    group = jnp.where(same, lane % half // FACET, -1)
    for at in range(FACET // 2):
        tile_ref[at] = jnp.where(group == at, 1.0, 0.0).astype(jnp.bfloat16)


def forward(bands, slots, here, arrive, ready, pay_ref, tile_ref, tab_ref, weight_ref, wide_ref, out_ref, mask, spread, plane, total):
    arrive(0)
    marks = pay_ref[0][:, PIXELS:].astype(jnp.float32)
    col_at = FACET * marks[:, 3:4] + marks[:, 4:5]
    spot = (lax.broadcasted_iota(jnp.int32, mask.shape, 1) % TW).astype(jnp.float32) - col_at
    mask[...] = jnp.where((spot >= 0.0) & (spot < FACET), 1.0, 0.0).astype(jnp.bfloat16)
    for part, side in ((0, 1), (1, 0)):
        if part:
            arrive(part)
        fields = pay_ref[part][:, :PIXELS]

        def widen(at, _, fields=fields, side=side):
            pixels = dot(fields, tile_ref[at]).astype(jnp.bfloat16) * mask[...]
            row = pl.multiple_of((side * (FACET // 2) + at) * slots, slots)
            for b in range(bands):
                spread[b, pl.ds(row, slots), :] = pixels[b * slots : (b + 1) * slots]
            return 0

        lax.fori_loop(0, FACET // 2, widen, 0)
    lane = lax.broadcasted_iota(jnp.int32, (8, 128), 1)
    select = jnp.where(lane == 1, float(FACET), jnp.where(lane == 2, 1.0, 0.0)).astype(jnp.bfloat16)
    group = 8
    depth = group * slots
    spot = lax.broadcasted_iota(jnp.int32, (TH, depth), 0).astype(jnp.float32)
    for b in range(bands):
        corner = pay_ref[0][b * slots : (b + 1) * slots, PIXELS:]
        row_at = lax.dot_general(
            select, corner, (((1,), (1,)), ((), ())), preferred_element_type=jnp.float32
        )[0:1]
        row_at = jnp.concatenate([row_at + float(u) for u in range(group)], axis=1)
        for at in range(FACET // group):
            hot = jnp.where(spot == row_at + float(at * group), 1.0, 0.0).astype(jnp.bfloat16)
            part = dot(hot, spread[b, at * depth : (at + 1) * depth, :])
            total[...] = part if at == 0 else total[...] + part
        plane[b] = total[...].astype(jnp.bfloat16)
    scale = 1.0 / math.sqrt(TH * TW)
    wide, rows = out_ref.shape[0], out_ref.shape[1] // 2
    chunk = max(rows, TH // 4)
    for start in range(0, TH, chunk):
        span = slice(start, start + chunk)
        table = jnp.concatenate([tab_ref[span, :], tab_ref[TH + start : TH + start + chunk, :]], axis=0)
        offsets = weight_ref[span, :]
        place = lax.broadcasted_iota(jnp.int32, offsets.shape, 1) - 2 * REACH
        both = None
        for b in range(bands):
            weight = jnp.sum(jnp.where(place == here - b, offsets, 0.0), axis=1, keepdims=True)
            term = jnp.concatenate([weight, weight], axis=0) * dot(table, plane[b])
            both = term if both is None else both + term
        real = both[:chunk, :TW] - both[chunk:, TW:]
        imag = both[:chunk, TW:] + both[chunk:, :TW]
        pair = jnp.concatenate([real, imag], axis=0).astype(jnp.bfloat16)
        spread_x = dot(pair, wide_ref[...])
        spec_r = (spread_x[:chunk, :TW] - spread_x[chunk:, TW:]) * scale
        spec_i = (spread_x[:chunk, TW:] + spread_x[chunk:, :TW]) * scale
        for w in range(start // rows, (start + chunk) // rows):
            part = slice(w * rows - start, (w + 1) * rows - start)
            out_ref[w] = jnp.concatenate([spec_r[part], spec_i[part]], axis=0).astype(jnp.bfloat16)
            ready(w)


def backward(
    wide, arrive, spec_ref, weight_ref, phase, wide_ref, high_ref, out_ref,
    parts, focus, back, image, send_a, recv_a, send_b, recv_b,
):
    column, band = lax.axis_index("wide"), lax.axis_index("narrow")
    rows = TH // wide

    def copy(step, source, landing, send, recv):
        there = lax.rem(column + step, wide)
        return pltpu.make_async_remote_copy(
            src_ref=source.at[there],
            dst_ref=landing.at[column],
            send_sem=send.at[step],
            recv_sem=recv.at[step],
            device_id=(there, band),
            device_id_type=MESH,
        )

    def out_copy(step):
        return copy(step, spec_ref, parts, send_a, recv_a)

    def home_copy(step):
        return copy(step, focus, back, send_b, recv_b)

    parts[column] = spec_ref[column]
    arrive()
    phase_r, phase_i = phase[0], phase[1]
    for step in range(1, wide):
        out_copy(step).wait_recv()
    for step in list(range(1, wide)) + [0]:
        there = lax.rem(column + step, wide)
        total = None
        for offset in range(-REACH, REACH + 1):
            source = there - offset
            inside = jnp.where((source >= 0) & (source < wide), 1.0, 0.0)
            weight = weight_ref[offset + REACH : offset + REACH + 1, :] * inside
            term = weight * parts[jnp.clip(source, 0, wide - 1)].astype(jnp.float32)
            total = term if total is None else total + term
        real, imag = total[:rows], total[rows:]
        turned = jnp.concatenate(
            [phase_r * real - phase_i * imag, phase_r * imag + phase_i * real], axis=0
        ).astype(jnp.bfloat16)
        if step:
            focus[there] = turned
            home_copy(step).start()
        else:
            back[column] = turned
    for step in range(wide):
        source = lax.rem(column - step + wide, wide)
        if step:
            home_copy(step).wait_recv()
        both = dot(back[source], wide_ref[...])
        top, low = both[:rows], both[rows:]
        image[source, :, :TW] = top[:, :TW] - low[:, TW:]
        image[source, :, TW:] = top[:, TW:] + low[:, :TW]
    scale = 1.0 / math.sqrt(TH * TW)
    pair = image[...].reshape(TH, 2 * TW).astype(jnp.bfloat16)
    top, low = dot(high_ref[:TH], pair), dot(high_ref[TH:], pair)
    out_ref[0] = (top[:, :TW] - low[:, TW:]) * scale
    out_ref[1] = (top[:, TW:] + low[:, :TW]) * scale
    for step in range(1, wide):
        out_copy(step).wait_send()
        home_copy(step).wait_send()


def whole_kernel(
    wide, narrow, bands, per,
    amp_ref, par_ref, row_weight, col_weight, fwd_w, inv_w, phase_all, fwd_h_all, inv_h_all, out_ref,
    gathered_a, gathered_b, outgoing_a, outgoing_b, incoming_a, incoming_b, send_n, recv_n, send_w, recv_w,
    pay_a, pay_b, tiles, mask, spread, plane, total, spec,
    parts, focus, back, image, send_a, recv_a, send_b, recv_b,
    phase, fwd_h, inv_h, load,
):
    column, band = lax.axis_index("wide"), lax.axis_index("narrow")
    rows = TH // wide
    own = pl.ds(pl.multiple_of(column * rows, rows), rows)
    fetch_tab = pltpu.make_async_copy(fwd_h_all, fwd_h, load.at[0])
    fetch_phase = pltpu.make_async_copy(phase_all.at[:, own, :], phase, load.at[1])
    fetch_inv = pltpu.make_async_copy(inv_h_all, inv_h, load.at[2])
    for one in (fetch_tab, fetch_phase, fetch_inv):
        one.start()
    pay = (pay_a, pay_b)
    landed, finish = front(
        wide, narrow, bands, per, lambda: fill_tiles(tiles), amp_ref, par_ref, pay,
        (gathered_a, gathered_b), (outgoing_a, outgoing_b), (incoming_a, incoming_b),
        send_n, recv_n, send_w, recv_w,
    )
    fetch_tab.wait()
    here = band - jnp.clip(band - REACH, 0, narrow - bands)

    def ready(w):
        step = lax.rem(w - column + wide, wide)

        @pl.when(step != 0)
        def _():
            pltpu.make_async_remote_copy(
                src_ref=spec.at[w],
                dst_ref=parts.at[column],
                send_sem=send_a.at[step],
                recv_sem=recv_a.at[step],
                device_id=(w, band),
                device_id_type=MESH,
            ).start()

    forward(
        bands, wide * per, here, landed, ready, pay, tiles, fwd_h, row_weight, fwd_w, spec, mask, spread, plane, total
    )

    def arrive():
        fetch_phase.wait()
        fetch_inv.wait()

    backward(
        wide, arrive, spec, col_weight, phase, inv_w, inv_h, out_ref,
        parts, focus, back, image, send_a, recv_a, send_b, recv_b,
    )
    finish()


def local(amplitude, tilt, owner, row_offset, col_offset):
    wide, narrow = lax.axis_size("wide"), lax.axis_size("narrow")
    facets = amplitude.shape[0]
    per = max(2, (3 * facets + wide - 1) // wide)
    bands = min(narrow, 2 * REACH + 1)
    slots = wide * per
    block = (bands * per + 15) // 16 * 16
    rows = TH // wide
    par = jnp.concatenate(
        [tilt, jnp.stack([owner[:, 0], row_offset, col_offset]).astype(jnp.float32)], axis=0
    )
    par = jnp.pad(par.T, ((0, 0), (0, 2)))
    row_weight = np.zeros((TH, 128), np.float32)
    col_weight = np.zeros((8, TW), np.float32)
    for offset in range(-REACH, REACH + 1):
        row_weight[:, 2 * REACH + offset] = reach_weight(TH, float(offset))
        col_weight[offset + REACH] = reach_weight(TW, float(offset))
    angle = depth_phase(TH)[:, None] + depth_phase(TW)[None, :]
    phase = np.stack([np.cos(angle), np.sin(angle)]).astype(np.float32)
    constants = [
        row_weight,
        col_weight,
        np.concatenate(dft_tables(TW, -1.0), axis=1),
        np.concatenate(dft_tables(TW, 1.0), axis=1),
        phase,
        np.concatenate(dft_tables(TH, -1.0), axis=0),
        np.concatenate(dft_tables(TH, 1.0), axis=0),
    ]
    dma = lambda *shape: pltpu.SemaphoreType.DMA(shape)
    narrow16 = lambda *shape: pltpu.VMEM(shape, jnp.bfloat16)
    wide32 = lambda *shape: pltpu.VMEM(shape, jnp.float32)
    return pl.pallas_call(
        functools.partial(whole_kernel, wide, narrow, bands, per),
        out_shape=jax.ShapeDtypeStruct((2, TH, TW), jnp.float32),
        in_specs=[pl.BlockSpec(memory_space=pltpu.VMEM)] * 6 + [pl.BlockSpec(memory_space=pl.ANY)] * 3,
        out_specs=pl.BlockSpec(memory_space=pltpu.VMEM),
        scratch_shapes=[
            *[narrow16(bands, facets, words) for words in PARTS],
            *[narrow16(wide, block, words) for words in PARTS],
            *[narrow16(wide, block, words) for words in PARTS],
            dma(2, 2 * REACH),
            dma(2, 2 * REACH),
            dma(2, wide),
            dma(2, wide),
            *[narrow16(bands * slots, words) for words in PARTS],
            narrow16(FACET // 2, PIXELS, 2 * TW),
            narrow16(bands * slots, 2 * TW),
            narrow16(bands, FACET * slots, 2 * TW),
            narrow16(bands, TH, 2 * TW),
            wide32(TH, 2 * TW),
            narrow16(wide, 2 * rows, TW),
            narrow16(wide, 2 * rows, TW),
            narrow16(wide, 2 * rows, TW),
            narrow16(wide, 2 * rows, TW),
            wide32(wide, rows, 2 * TW),
            dma(wide),
            dma(wide),
            dma(wide),
            dma(wide),
            wide32(2, rows, TW),
            narrow16(2 * TH, TH),
            narrow16(2 * TH, TH),
            dma(3),
        ],
        compiler_params=pltpu.CompilerParams(
            collective_id=0, has_side_effects=True, vmem_limit_bytes=56 * 2**20
        ),
    )(amplitude, par, *[jnp.asarray(one) for one in constants])


def solution(mesh):
    in_specs = (
        P(("wide", "narrow"), None),
        P(None, ("wide", "narrow")),
        P(("wide", "narrow"), None),
        P(("wide", "narrow")),
        P(("wide", "narrow")),
    )
    out_specs = P(None, "narrow", "wide")
    return jax.shard_map(local, mesh=mesh, in_specs=in_specs, out_specs=out_specs, check_vma=False)
```
